32 devices in a mesh: group: 2 (over y), expert: 4 (over z), dp: 4 (over x, core).
Axes of the slice: x: 2, y: 2, z: 4, core: 2. Of those that a mesh axis runs over, the one named last changes fastest.
Arguments:
- tokens: bfloat16 [256, 4096], P(('group', 'expert', 'dp')), parts along dimension 0, may hold values from -6 to 6
- routing: int32 [256, 8], P(('group', 'expert', 'dp')), parts along dimension 0, may hold values from 0 to 127, as said below
- gate_quantized: int32 [256, 8], P(('group', 'expert', 'dp')), parts along dimension 0, may hold values from 1 to 32767
- tenant: int32 [256], P(('group', 'expert', 'dp')), parts along dimension 0, may hold values from 0 to 23
- tenant_page_lookup: int32 [4, 24], replicated, may hold values from 0 to 23, each once within a row
- gate_weight: bfloat16 [4, 4096, 1024], P('expert', None, 'dp'), may hold values from -0.09375 to 0.09375
- up_projection: bfloat16 [4, 4096, 1024], P('expert', None, 'dp'), may hold values from -0.09375 to 0.09375
- down_weight: bfloat16 [4, 1024, 4096], P('expert', None, 'dp'), may hold values from -0.1875 to 0.1875
- adapter_shrink: bfloat16 [4, 24, 16, 4096], P('expert', 'dp'), may hold values from -0.09375 to 0.09375
- adapter_expand: bfloat16 [4, 24, 16, 1024], P('expert', 'dp'), may hold values from -1.5 to 1.5
Outputs:
- mixed_out: bfloat16 [256, 4096], P(('group', 'expert', 'dp')), parts along dimension 0
The draws below stay inside these ranges and needn't reach their ends.
There are 2 independent parts, one for each index of `group`. The reference program is written for one: setup_inputs(seed, part) draws one part's arguments, and reference() takes and returns one part's arrays. A program takes and returns all parts, laid end to end along the dimension named above; an argument that names none is the same for every part. Nothing has to cross between parts.
Inputs may be any that keep to these rules, and one draw needn't show every extreme that they name: `routing`: each row names 8 different experts. Among the 8 tokens of one device no expert is named more than 2 times, and in every draw some expert below 4 is named exactly 2 times by the tokens of every device. `tenant_page_lookup`: row e gives every tenant a different page of expert e's pool.
All inputs are finite; a program needn't handle non-finite values.
Results may differ from the reference program's by a relative error of at most 0.0061.
Values may be sent and summed in bfloat16 or wider, within the bound.
No kernel may reach another device: no remote copies, remote signals or barrier semaphores. Data moves between devices by JAX's collectives and lax.ppermute only.
A program may use at most 64 MiB of HBM per device.

```python
import jax
import jax.numpy as jnp
from jax import lax

MODEL_DIMENSION = 4096
EXPERT_HIDDEN = 1024
EXPERTS_ALL = 128
TOPK = 8
ADAPTER_RANK = 16
TENANT_COUNT = 24
TOK_DEV = 8
FLIGHT_EXPERTS = 4
TOKENS = 128
N_EXPERT = 4
N_DP = 4


def draw_routing(key, part):
    unit = TOK_DEV // 8
    loaded_base = jnp.concatenate([jnp.full((16,), 2 * unit, jnp.int32), jnp.full((32,), unit, jnp.int32)])
    hottest = jax.random.randint(jax.random.fold_in(key, 11), (), 0, FLIGHT_EXPERTS)
    block_total = TOKENS // TOK_DEV
    places = jnp.arange(TOK_DEV * TOPK, dtype=jnp.int32)
    all_ids = jnp.arange(EXPERTS_ALL, dtype=jnp.int32)

    def one_block(block_key):
        first_key, second_key, third_key = jax.random.split(block_key, 3)
        shuffled_ids = jax.random.permutation(first_key, EXPERTS_ALL).astype(jnp.int32)
        order_key = jnp.where(shuffled_ids < FLIGHT_EXPERTS, 0, EXPERTS_ALL).astype(jnp.int32) + all_ids
        ordered_ids = shuffled_ids[jnp.argsort(order_key, stable=True)]
        loaded = loaded_base[jax.random.permutation(third_key, 48)]
        loaded_full = jnp.concatenate([loaded, jnp.zeros((EXPERTS_ALL - 48,), jnp.int32)])
        loads = jnp.zeros((EXPERTS_ALL,), jnp.int32).at[ordered_ids].set(loaded_full)
        where_full = jnp.argmax((loads == 2 * unit).astype(jnp.int32))
        loads = loads.at[where_full].set(loads[hottest]).at[hottest].set(2 * unit)
        ends = jnp.cumsum(loads)
        listed = jnp.sum((ends[None, :] <= places[:, None]).astype(jnp.int32), axis=1)
        chosen = listed.reshape(TOPK, TOK_DEV).T
        shuffle = jax.random.permutation(second_key, TOK_DEV)
        return chosen[shuffle]
    block_keys = jax.random.split(jax.random.fold_in(key, 5), block_total)
    return jax.vmap(one_block)(block_keys).reshape(TOKENS, TOPK).astype(jnp.int32)


def set_ends(entries, own_key, least, high):
    extent = entries.shape
    spot = [jax.random.randint(jax.random.fold_in(own_key, axis), (), 0, extent[axis]) for axis in range(len(extent))]
    entries = entries.at[tuple(spot)].set(least)
    longest = extent.index(max(extent))
    spot[longest] = (spot[longest] + 1) % extent[longest]
    return entries.at[tuple(spot)].set(high)


def steps_of(rng, dims, cuts, smallest, high):
    factor_of = 1.0
    for dim, shards_of in cuts:
        draws = jax.random.uniform(jax.random.fold_in(jax.random.fold_in(rng, 6), dim), (shards_of,), jnp.float32, smallest / len(cuts), high / len(cuts))
        factor_of = factor_of * jnp.repeat(jnp.exp(draws), dims[dim] // shards_of).reshape((-1,) + (1,) * (len(dims) - 1 - dim))
    return factor_of


def scatter_about(key, extent, deviation, reach, shards=(), held_as=jnp.bfloat16):
    values = deviation * jax.random.normal(key, extent, jnp.float32)
    if shards:
        values = values * steps_of(key, extent, shards, -0.22, 0.18)
    return jnp.clip(values, -reach, reach).astype(held_as)


def setup_inputs(seed: int = 0, part: int = 0) -> dict:
    seeds = jax.random.split(jax.random.key(seed), 11)
    part_keys = jax.random.split(jax.random.fold_in(seeds[10], part), 11)
    return {
        "tokens": scatter_about(part_keys[0], (TOKENS, MODEL_DIMENSION), 1.0, 6.0, ((0, 16),)),
        "routing": draw_routing(jax.random.fold_in(jax.random.fold_in(seeds[10], part), 71), part),
        "gate_quantized": set_ends(jax.random.randint(part_keys[2], (TOKENS, TOPK), 1, 32768), jax.random.fold_in(part_keys[2], 1), 1, 32767).astype(jnp.int32),
        "tenant": set_ends(jax.random.randint(part_keys[3], (TOKENS,), 0, TENANT_COUNT), jax.random.fold_in(part_keys[3], 1), 0, TENANT_COUNT - 1).astype(jnp.int32),
        "tenant_page_lookup": jax.vmap(lambda own: jax.random.permutation(own, TENANT_COUNT))(jax.random.split(seeds[4], FLIGHT_EXPERTS)).reshape((FLIGHT_EXPERTS, TENANT_COUNT)).astype(jnp.int32),
        "gate_weight": scatter_about(seeds[5], (FLIGHT_EXPERTS, MODEL_DIMENSION, EXPERT_HIDDEN), MODEL_DIMENSION ** -0.5, 0.09375, ((0, 4), (2, 4))),
        "up_projection": scatter_about(seeds[6], (FLIGHT_EXPERTS, MODEL_DIMENSION, EXPERT_HIDDEN), MODEL_DIMENSION ** -0.5, 0.09375, ((0, 4), (2, 4))),
        "down_weight": scatter_about(seeds[7], (FLIGHT_EXPERTS, EXPERT_HIDDEN, MODEL_DIMENSION), EXPERT_HIDDEN ** -0.5, 0.1875, ((0, 4), (2, 4))),
        "adapter_shrink": scatter_about(seeds[8], (FLIGHT_EXPERTS, TENANT_COUNT, ADAPTER_RANK, MODEL_DIMENSION), MODEL_DIMENSION ** -0.5, 0.09375, ((0, 4), (1, 4))),
        "adapter_expand": scatter_about(seeds[9], (FLIGHT_EXPERTS, TENANT_COUNT, ADAPTER_RANK, EXPERT_HIDDEN), ADAPTER_RANK ** -0.5, 1.5, ((0, 4), (1, 4))),
    }


def reference(tokens, routing, gate_quantized, tenant, tenant_page_lookup, gate_weight, up_projection, down_weight, adapter_shrink, adapter_expand):
    devices_all = N_EXPERT * N_DP
    capacity = TOK_DEV // 4
    slot_total = devices_all * capacity
    expert_ids = jnp.arange(FLIGHT_EXPERTS, dtype=jnp.int32)
    matches = routing[:, :, None] == expert_ids[None, None, :]
    assign = jnp.sum(matches.astype(jnp.int32), axis=1)
    mix_coef = jnp.sum(jnp.where(matches, gate_quantized[:, :, None].astype(jnp.float32) / 32768.0, jnp.float32(0.0)), axis=1)
    blocked = assign.reshape(devices_all, TOK_DEV, FLIGHT_EXPERTS)
    slot_rank = (jnp.cumsum(blocked, axis=1) - blocked).reshape(TOKENS, FLIGHT_EXPERTS)
    token_ids = jnp.arange(TOKENS, dtype=jnp.int32)
    source = token_ids // TOK_DEV
    slot_of = jnp.where(assign == 1, source[:, None] * capacity + slot_rank, slot_total).astype(jnp.int32)

    def one_expert(running, expert_number):
        slot_here = lax.dynamic_index_in_dim(slot_of, expert_number, 1, keepdims=False)
        holder = jnp.full((slot_total,), TOKENS, jnp.int32).at[slot_here].set(token_ids, mode="drop")
        occupied = holder < TOKENS
        safe_ids = jnp.minimum(holder, TOKENS - 1).astype(jnp.int32)
        slot_input = jnp.where(occupied[:, None], tokens[safe_ids], jnp.zeros((), tokens.dtype))
        page_row = lax.dynamic_index_in_dim(tenant_page_lookup, expert_number, 0, keepdims=False)
        page_numbers = page_row[tenant[safe_ids]].astype(jnp.int32)
        shrink_weight = lax.dynamic_index_in_dim(adapter_shrink, expert_number, 0, keepdims=False)
        products = jnp.dot(slot_input, shrink_weight.reshape(TENANT_COUNT * ADAPTER_RANK, MODEL_DIMENSION).T, preferred_element_type=jnp.float32)
        products = products.reshape(slot_total, TENANT_COUNT, ADAPTER_RANK)
        shrink_result = jnp.take_along_axis(products, page_numbers[:, None, None], axis=1)[:, 0, :].astype(jnp.bfloat16)
        expand_weight = lax.dynamic_index_in_dim(adapter_expand, expert_number, 0, keepdims=False)[page_numbers]
        adapter_update = jnp.einsum("cz,czy->cy", shrink_result.astype(jnp.float32), expand_weight.astype(jnp.float32))
        gate_w = lax.dynamic_index_in_dim(gate_weight, expert_number, 0, keepdims=False)
        up_weight = lax.dynamic_index_in_dim(up_projection, expert_number, 0, keepdims=False)
        down_w = lax.dynamic_index_in_dim(down_weight, expert_number, 0, keepdims=False)
        gate_act = jnp.dot(slot_input, gate_w, preferred_element_type=jnp.float32)
        up_activation = jnp.dot(slot_input, up_weight, preferred_element_type=jnp.float32) + adapter_update
        hidden = (jax.nn.silu(gate_act) * up_activation).astype(jnp.bfloat16)
        expert_out = jnp.dot(hidden, down_w, preferred_element_type=jnp.float32).astype(jnp.bfloat16)
        coef_here = lax.dynamic_index_in_dim(mix_coef, expert_number, 1, keepdims=False)[safe_ids]
        weight_here = jnp.where(occupied, coef_here, jnp.float32(0.0))
        running = running.at[safe_ids].add(weight_here[:, None] * expert_out.astype(jnp.float32))
        return running, None

    mixed_out, unused = lax.scan(one_expert, jnp.zeros((TOKENS, MODEL_DIMENSION), jnp.float32), expert_ids)
    return mixed_out.astype(jnp.bfloat16)
```

```python
import jax
import jax.numpy as jnp
from jax import lax
from jax.sharding import PartitionSpec as P

BF = jnp.bfloat16
F32 = jnp.float32


def swap(x, axis, size, mask):
    return lax.ppermute(x, axis, [(i, i ^ mask) for i in range(size)])


def bits_of(size):
    return [1 << b for b in range(size.bit_length() - 1)]


def gather_order(size):
    order = [0]
    for mask in reversed(bits_of(size)):
        order = order + [q ^ mask for q in order]
    return order


def gather_rows(x, axis, size):
    x = x[None]
    for mask in reversed(bits_of(size)):
        x = jnp.concatenate([x, swap(x, axis, size, mask)], axis=0)
    return x


def exchange(x, axis, size, dim, order):
    for mask in bits_of(size):
        keep = [i for i in range(size) if not order[i] & mask]
        send = [order.index(order[i] ^ mask) for i in keep]
        kept = jnp.stack([lax.index_in_dim(x, i, dim, False) for i in keep], dim)
        sent = jnp.stack([lax.index_in_dim(x, i, dim, False) for i in send], dim)
        came = swap(sent, axis, size, mask)
        parts = [None] * size
        for j in range(size // 2):
            parts[keep[j]] = lax.index_in_dim(kept, j, dim, False)
            parts[send[j]] = lax.index_in_dim(came, j, dim, False)
        x = jnp.stack(parts, dim)
    return x


def build(mesh):
    n_exp, n_dp = mesh.shape["expert"], mesh.shape["dp"]
    order_e = list(range(n_exp))
    order_d = gather_order(n_dp)

    def per_device(
        tokens,
        routing,
        gate_quantized,
        tenant,
        tenant_page_lookup,
        gate_weight,
        up_projection,
        down_weight,
        adapter_shrink,
        adapter_expand,
    ):
        tok_count, width = tokens.shape
        experts, tenants = tenant_page_lookup.shape
        cap = tok_count // 4
        pages, rank = adapter_shrink.shape[1:3]
        hid = gate_weight.shape[2]
        part = down_weight.shape[2]
        mine = lax.axis_index("expert")
        col = lax.axis_index("dp")

        expand = gather_rows(
            adapter_expand.reshape(pages * rank, adapter_expand.shape[3]), "dp", n_dp
        ).reshape(n_dp * pages * rank, adapter_expand.shape[3])

        ids = jnp.arange(experts, dtype=jnp.int32) ^ mine
        matches = routing[:, :, None] == ids[None, None, :]
        assign = jnp.any(matches, axis=1)
        toks = jnp.arange(tok_count, dtype=jnp.int32)
        earlier = toks[:, None] > toks[None, :]
        slot_rank = jnp.sum((earlier[:, :, None] & assign[None, :, :]).astype(jnp.int32), axis=1)
        caps = jnp.arange(cap, dtype=jnp.int32)
        placing = assign[:, :, None] & (slot_rank[:, :, None] == caps[None, None, :])
        coef = jnp.sum(jnp.where(matches, gate_quantized[:, :, None].astype(F32) / 32768.0, 0.0), axis=1)
        mix = jnp.where(placing, coef[:, :, None], 0.0).reshape(tok_count, experts * cap)
        place = placing.reshape(tok_count, experts * cap)
        rows = lax.dot_general(
            place.astype(BF), tokens, (((0,), (0,)), ((), ())), preferred_element_type=F32
        ).astype(BF)
        hot = tenant[:, None] == jnp.arange(tenants, dtype=jnp.int32)[None, :]
        looked = jnp.sum(
            jnp.where(hot[:, None, :], tenant_page_lookup[None, :, :], 0), axis=2
        )
        looked = jnp.sum(
            jnp.where(
                jnp.arange(experts)[None, None, :] == ids[None, :, None], looked[:, None, :], 0
            ),
            axis=2,
        )
        slot_page = jnp.sum(jnp.where(placing, looked[:, :, None], 0), axis=0).reshape(-1)
        tail = jnp.broadcast_to(slot_page[:, None].astype(BF), (experts * cap, 128))
        sent = jnp.concatenate([rows, tail], axis=1).reshape(experts, cap, width + 128)

        got = exchange(sent, "expert", n_exp, 0, order_e)
        got = gather_rows(got, "dp", n_dp).reshape(-1, width + 128)
        slots = got[:, :width]
        page = got[:, width].astype(jnp.int32)

        gate = jnp.dot(slots, gate_weight[0], preferred_element_type=F32)
        up = jnp.dot(slots, up_projection[0], preferred_element_type=F32)
        prod = lax.dot_general(
            slots,
            adapter_shrink.reshape(pages * rank, width),
            (((1,), (1,)), ((), ())),
            preferred_element_type=F32,
        )
        page_of = col * pages + jnp.arange(pages * rank, dtype=jnp.int32) // rank
        masked = jnp.where(page[:, None] == page_of[None, :], prod, 0.0)
        packed = jnp.concatenate(
            [jax.nn.silu(gate).astype(BF), up.astype(BF), masked.astype(BF)], axis=1
        )
        block = experts * cap
        every = [packed]
        for mask in reversed(bits_of(n_dp)):
            flat = jnp.concatenate(every, axis=1) if len(every) > 1 else every[0]
            came = swap(flat, "dp", n_dp, mask)
            came = came.reshape(n_dp, block, -1)
            came = jnp.stack([came[order_d.index(q ^ mask)] for q in order_d])
            came = came.reshape(n_dp * block, -1)
            every = every + jnp.split(came, len(every), axis=1)
        wide = pages * rank
        silus = jnp.stack([y[:, :hid] for y in every])
        ups = jnp.stack([y[:, hid : 2 * hid] for y in every])
        low = jnp.concatenate([y[:, 2 * hid :] for y in every], axis=1)

        def absolute(x):
            x = jnp.stack([x[order_d.index(j)] for j in range(n_dp)])
            for mask in bits_of(n_dp):
                turned = jnp.stack([x[j ^ mask] for j in range(n_dp)])
                x = jnp.where((col & mask) != 0, turned, x)
            return x

        silus, ups = absolute(silus), absolute(ups)
        silus = jnp.moveaxis(silus, 0, 1).reshape(n_dp * block, n_dp * hid)
        ups = jnp.moveaxis(ups, 0, 1).reshape(n_dp * block, n_dp * hid)
        add = jnp.dot(low, expand, preferred_element_type=F32)
        hidden = (silus.astype(F32) * (ups.astype(F32) + add)).astype(BF)
        out = jnp.dot(hidden, down_weight[0], preferred_element_type=F32).astype(BF)
        out = out.reshape(n_dp, experts, cap, part)
        out = exchange(out, "dp", n_dp, 0, order_d)
        out = exchange(out, "expert", n_exp, 1, order_e)
        out = out.reshape(n_dp, block, part).astype(F32)
        mixed = jnp.sum(mix[None, :, :, None] * out[:, None, :, :], axis=2).astype(BF)
        mixed = absolute(mixed)
        return jnp.moveaxis(mixed, 0, 1).reshape(tok_count, n_dp * part)

    return per_device


def solution(mesh):
    row = ("group", "expert", "dp")
    return jax.shard_map(
        build(mesh),
        mesh=mesh,
        in_specs=(
            P(row, None),
            P(row, None),
            P(row, None),
            P(row),
            P(),
            P("expert", None, "dp"),
            P("expert", None, "dp"),
            P("expert", None, "dp"),
            P("expert", "dp", None, None),
            P("expert", "dp", None, None),
        ),
        out_specs=P(row, None),
        check_vma=False,
    )
```

```python
import jax
import jax.numpy as jnp
from jax import lax
from jax.experimental import pallas as pl
from jax.experimental.pallas import tpu as pltpu
from jax.sharding import PartitionSpec as P

BF = jnp.bfloat16
F32 = jnp.float32
I32 = jnp.int32
TAIL = 128
VM = pl.BlockSpec(memory_space=pltpu.VMEM)
HB = pl.BlockSpec(memory_space=pl.ANY)


def swap(x, axis, size, mask):
    return lax.ppermute(x, axis, [(i, i ^ mask) for i in range(size)])


def bits_of(size):
    return [1 << b for b in range(size.bit_length() - 1)]


def gather_order(size):
    order = [0]
    for mask in reversed(bits_of(size)):
        order = order + [q ^ mask for q in order]
    return order


def turned(x, col, size, names_in, names_out):
    rows = x.shape[0] // size
    block = {q: x[i * rows : (i + 1) * rows] for i, q in enumerate(names_in)}
    for mask in bits_of(size):
        here = (col & mask) != 0
        block = {q: jnp.where(here, block[q ^ mask], block[q]) for q in range(size)}
    return jnp.concatenate([block[q] for q in names_out], axis=0)


def slot_kernel(topk, tok_ref, meta_ref, sent_ref, mix_ref):
    tok_count, width = tok_ref.shape
    experts, lanes = meta_ref.shape[0] - 3 * tok_count, meta_ref.shape[1]
    slots = sent_ref.shape[0]
    cap = slots // experts
    mine = lax.axis_index("expert")
    lane = lax.broadcasted_iota(I32, (tok_count, slots), 1)
    expert_of = (lane // cap) ^ mine
    routing = meta_ref[:tok_count]
    quant = meta_ref[tok_count : 2 * tok_count].astype(F32) * (1.0 / 32768.0)
    assign = jnp.zeros((tok_count, slots), F32)
    coef = jnp.zeros((tok_count, slots), F32)
    for k in range(topk):
        match = routing[:, k : k + 1] == expert_of
        assign = jnp.where(match, 1.0, assign)
        coef = jnp.where(match, quant[:, k : k + 1], coef)
    below = lax.broadcasted_iota(I32, (tok_count, tok_count), 0) > lax.broadcasted_iota(
        I32, (tok_count, tok_count), 1
    )
    slot_rank = jnp.dot(
        jnp.where(below, 1.0, 0.0).astype(BF), assign.astype(BF), preferred_element_type=F32
    )
    place = jnp.where(slot_rank == (lane % cap).astype(F32), assign, 0.0)
    mix_ref[...] = place * coef
    who = meta_ref[2 * tok_count : 2 * tok_count + 1][:, :tok_count]
    hot = jnp.where(lax.broadcasted_iota(I32, (lanes, tok_count), 0) == who, 1.0, 0.0)
    pages = lax.dot_general(
        hot.astype(BF),
        meta_ref[3 * tok_count :].astype(F32).astype(BF),
        (((0,), (1,)), ((), ())),
        preferred_element_type=F32,
    )
    pick = jnp.where(
        lax.broadcasted_iota(I32, (experts, slots), 0)
        == (lax.broadcasted_iota(I32, (experts, slots), 1) // cap) ^ mine,
        1.0,
        0.0,
    )
    page = place * jnp.dot(pages.astype(BF), pick.astype(BF), preferred_element_type=F32)
    by_token = (((0,), (0,)), ((), ()))
    sent_ref[:, :width] = lax.dot_general(
        place.astype(BF), tok_ref[...], by_token, preferred_element_type=F32
    ).astype(BF)
    sent_ref[:, width:] = lax.dot_general(
        page.astype(BF), jnp.ones((tok_count, TAIL), BF), by_token, preferred_element_type=F32
    ).astype(BF)


def expert_kernel(n_dp, rank, own_ref, came_ref, gate_ref, up_ref, shrink_ref, expand_ref, out_ref):
    width = gate_ref.shape[0]
    hid = gate_ref.shape[1]
    wide = shrink_ref.shape[0]
    col = lax.axis_index("dp")
    x = jnp.concatenate([own_ref[:, :width], came_ref[:, :width]], axis=0)
    page = jnp.concatenate([own_ref[:, width:], came_ref[:, width:]], axis=0).astype(F32)[:, :1]
    rows = x.shape[0]
    order = gather_order(n_dp)
    prod = lax.dot_general(
        x, shrink_ref[...], (((1,), (1,)), ((), ())), preferred_element_type=F32
    )
    page_of = col * (wide // rank) + lax.broadcasted_iota(I32, (rows, wide), 1) // rank
    masked = jnp.where(page == page_of.astype(F32), prod, 0.0).astype(BF)
    grown = jnp.dot(masked, expand_ref[...], preferred_element_type=F32)
    gate = jnp.dot(x, gate_ref[...], preferred_element_type=F32)
    up = jnp.dot(x, up_ref[...], preferred_element_type=F32)
    act = gate / (1.0 + jnp.exp(-gate))

    def put(at, y):
        y = turned(y, col, n_dp, order, list(range(n_dp)))
        out_ref[:, at : at + y.shape[1]] = y.astype(BF)

    put(0, act)
    put(hid, act * up)
    put(2 * hid, grown)


def down_kernel(n_dp, hid, own_ref, came_ref, down_ref, keep_ref, send_ref, add_ref):
    col = lax.axis_index("dp")
    order = gather_order(n_dp)
    half = n_dp // 2
    split = 2 * hid * half
    rows = own_ref.shape[0]
    block = rows // n_dp
    part = down_ref.shape[1]
    add_ref[...] = own_ref[:, split:].astype(F32) + came_ref[:, split:].astype(F32)
    total = jnp.zeros((2 * rows, part), F32)
    for i, p in enumerate(order):
        ref = own_ref if i < half else came_ref
        at = (i % half) * 2 * hid
        start = pl.multiple_of((p ^ col) * hid, hid)
        act = ref[:, at : at + hid]
        first = ref[:, at + hid : at + 2 * hid]
        second = (act.astype(F32) * add_ref[:, pl.ds(start, hid)]).astype(BF)
        both = jnp.concatenate([first, second], axis=0)
        total += jnp.dot(both, down_ref[pl.ds(start, hid), :], preferred_element_type=F32)
    out = total[:rows] + total[rows:]
    out = turned(out, col, n_dp, list(range(n_dp)), order)
    for i in range(n_dp):
        ref = keep_ref if i < half else send_ref
        at = (i % half) * part
        ref[:, at : at + part] = out[i * block : (i + 1) * block].astype(BF)


def mix_kernel(n_dp, part, mix_ref, kept_ref, came_ref, out_ref):
    col = lax.axis_index("dp")
    mix = mix_ref[...]
    blocks, cap = kept_ref.shape[:2]
    for p in range(n_dp):
        lanes = slice(p * part, (p + 1) * part)
        total = jnp.zeros((mix.shape[0], part), F32)
        for i, ref in enumerate((kept_ref, came_ref)):
            for r in range(blocks):
                x = ref[r, :, lanes].astype(F32)
                for c in range(cap):
                    at = (i * blocks + r) * cap + c
                    total += mix[:, at : at + 1] * x[c : c + 1]
        out_ref[:, pl.ds(pl.multiple_of((p ^ col) * part, part), part)] = total.astype(BF)


def hold_kernel(x_ref, *refs):
    refs[-1][...] = x_ref[...]


def hold(x, *arrays):
    return call(
        hold_kernel,
        jax.ShapeDtypeStruct(x.shape, x.dtype),
        0,
        in_specs=[VM] + [HB] * len(arrays),
    )(x, *arrays)


def call(kernel, out_shape, n_in, limit=4 << 20, **kw):
    specs = kw.pop("in_specs", [VM] * n_in)
    outs = jax.tree.map(lambda _: VM, out_shape)
    return pl.pallas_call(
        kernel,
        out_shape=out_shape,
        in_specs=specs,
        out_specs=outs,
        compiler_params=pltpu.CompilerParams(vmem_limit_bytes=limit),
        **kw,
    )


def build(mesh):
    n_exp, n_dp = mesh.shape["expert"], mesh.shape["dp"]

    def stage(blocks, axis, size, mask, dim, early=()):
        labels = sorted(blocks)
        sent = [q for q in labels if q & mask]
        x = jnp.concatenate([blocks[q] for q in sent], axis=dim)
        came = jnp.split(swap(x, axis, size, mask), len(sent), axis=dim)
        if early:
            stay = [q for q in labels if not q & mask]
            x = hold(jnp.concatenate([blocks[q] for q in stay], axis=dim), *early)
            blocks = {**blocks, **dict(zip(stay, jnp.split(x, len(stay), axis=dim)))}
        return {**blocks, **dict(zip(sent, came))}

    def per_device(
        tokens,
        routing,
        gate_quantized,
        tenant,
        tenant_page_lookup,
        gate_weight,
        up_projection,
        down_weight,
        adapter_shrink,
        adapter_expand,
    ):
        tok_count, width = tokens.shape
        experts = tenant_page_lookup.shape[0]
        cap = tok_count // 4
        pages, rank = adapter_shrink.shape[1:3]
        hid = gate_weight.shape[2]
        hidden_all = adapter_expand.shape[3]
        part = down_weight.shape[2]
        block = experts * cap
        rows = n_dp * block
        half = n_dp // 2
        shape = jax.ShapeDtypeStruct
        topk = routing.shape[1]
        lanes = max(tenant_page_lookup.shape[1], topk, tok_count)

        def wide(x, rows):
            return jnp.pad(x, ((0, rows - x.shape[0]), (0, lanes - x.shape[1])))

        meta = jnp.concatenate(
            [
                wide(routing, tok_count),
                wide(gate_quantized, tok_count),
                wide(tenant[None], tok_count),
                wide(tenant_page_lookup, experts),
            ],
            axis=0,
        )
        sent, mix = call(
            lambda *refs: slot_kernel(topk, *refs),
            (shape((block, width + TAIL), BF), shape((tok_count, block), F32)),
            2,
        )(tokens, meta)

        state = sent.reshape(n_exp, cap, width + TAIL)
        state = {r: state[r : r + 1] for r in range(n_exp)}
        gate_w = gate_weight.reshape(width, hid)
        up_w = up_projection.reshape(width, hid)
        shrink_w = adapter_shrink.reshape(pages * rank, width)
        expand_w = adapter_expand.reshape(pages * rank, hidden_all)
        early = [(gate_w,), (gate_w, up_w)]
        for mask in bits_of(n_exp):
            state = stage(state, "expert", n_exp, mask, 0, early.pop(0) if early else ())
        own = jnp.concatenate([state[r] for r in range(n_exp)], axis=0)
        own = own.reshape(block, width + TAIL)
        masks = list(reversed(bits_of(n_dp)))
        for mask in masks[:-1]:
            other = swap(own, "dp", n_dp, mask)
            own = jnp.concatenate([hold(own, gate_w, up_w, shrink_w, expand_w), other], axis=0)
        came = swap(own, "dp", n_dp, masks[-1])
        packed = call(
            lambda *refs: expert_kernel(n_dp, rank, *refs),
            shape((rows, 2 * hid + hidden_all), BF),
            6,
        )(
            own,
            came,
            gate_w,
            up_w,
            shrink_w,
            expand_w,
        )

        for mask in masks[:-1]:
            other = swap(packed, "dp", n_dp, mask)
            at = packed.shape[1] - hidden_all
            packed = jnp.concatenate(
                [packed[:, :at], other[:, :at], packed[:, at:] + other[:, at:]], axis=1
            )
        other = swap(packed, "dp", n_dp, masks[-1])
        keep, send = call(
            lambda *refs: down_kernel(n_dp, hid, *refs),
            (shape((block, half * part), BF),) * 2,
            3,
            scratch_shapes=[pltpu.VMEM((rows, hidden_all), F32)],
        )(packed, other, down_weight.reshape(-1, part))

        back = swap(send, "dp", n_dp, 1)
        order = gather_order(n_dp)
        state = {}
        for i, q in enumerate(order[:half]):
            state[q] = keep[:, i * part : (i + 1) * part]
            state[q ^ 1] = back[:, i * part : (i + 1) * part]
        for mask in bits_of(n_dp)[1:]:
            state = stage(state, "dp", n_dp, mask, 1)
        home = jnp.concatenate([state[q] for q in range(n_dp)], axis=1)
        home = home.reshape(n_exp, cap, n_dp * part)
        state = {r: home[r : r + 1] for r in range(n_exp)}
        for mask in bits_of(n_exp)[:-1]:
            state = stage(state, "expert", n_exp, mask, 0)
        middle = n_exp // 2
        kept = jnp.concatenate([state[r] for r in range(middle)], axis=0)
        sent = jnp.concatenate([state[r] for r in range(middle, n_exp)], axis=0)
        came = swap(sent, "expert", n_exp, middle)
        return call(
            lambda *refs: mix_kernel(n_dp, part, *refs),
            shape((tok_count, n_dp * part), BF),
            3,
        )(mix, kept, came)

    return per_device


def solution(mesh):
    row = ("group", "expert", "dp")
    return jax.shard_map(
        build(mesh),
        mesh=mesh,
        in_specs=(
            P(row, None),
            P(row, None),
            P(row, None),
            P(row),
            P(),
            P("expert", None, "dp"),
            P("expert", None, "dp"),
            P("expert", None, "dp"),
            P("expert", "dp", None, None),
            P("expert", "dp", None, None),
        ),
        out_specs=P(row, None),
        check_vma=False,
    )
```

```python
import jax
import jax.numpy as jnp
from jax import lax
from jax.experimental import pallas as pl
from jax.experimental.pallas import tpu as pltpu
from jax.sharding import PartitionSpec as P

BF = jnp.bfloat16
F32 = jnp.float32
I32 = jnp.int32
TAIL = 128
VM = pl.BlockSpec(memory_space=pltpu.VMEM)
HB = pl.BlockSpec(memory_space=pl.ANY)


def swap(x, axis, size, mask):
    return lax.ppermute(x, axis, [(i, i ^ mask) for i in range(size)])


def bits_of(size):
    return [1 << b for b in range(size.bit_length() - 1)]


def gather_order(size):
    order = [0]
    for mask in reversed(bits_of(size)):
        order = order + [q ^ mask for q in order]
    return order


def turned(x, col, size, names_in, names_out):
    rows = x.shape[0] // size
    block = {q: x[i * rows : (i + 1) * rows] for i, q in enumerate(names_in)}
    for mask in bits_of(size):
        here = (col & mask) != 0
        block = {q: jnp.where(here, block[q ^ mask], block[q]) for q in range(size)}
    return jnp.concatenate([block[q] for q in names_out], axis=0)


def slot_kernel(
    tok_ref, routing_ref, gate_ref, tenant_ref, lookup_ref, keep_ref, send_ref, mix_ref
):
    tok_count, width = tok_ref.shape
    experts, tenants = lookup_ref.shape
    slots = mix_ref.shape[1]
    cap = slots // experts
    topk = routing_ref.shape[1]
    mine = lax.axis_index("expert")
    lane = lax.broadcasted_iota(I32, (tok_count, slots), 1)
    expert_of = (lane // cap) ^ mine
    routing = routing_ref[...]
    quant = gate_ref[...].astype(F32) * (1.0 / 32768.0)
    assign = jnp.zeros((tok_count, slots), F32)
    coef = jnp.zeros((tok_count, slots), F32)
    for k in range(topk):
        match = routing[:, k : k + 1] == expert_of
        assign = jnp.where(match, 1.0, assign)
        coef = jnp.where(match, quant[:, k : k + 1], coef)
    below = lax.broadcasted_iota(I32, (tok_count, tok_count), 0) > lax.broadcasted_iota(
        I32, (tok_count, tok_count), 1
    )
    slot_rank = jnp.dot(
        jnp.where(below, 1.0, 0.0).astype(BF), assign.astype(BF), preferred_element_type=F32
    )
    place = jnp.where(slot_rank == (lane % cap).astype(F32), assign, 0.0)
    mix_ref[...] = place * coef
    row = lax.broadcasted_iota(I32, (tok_count, tenants), 0)
    who = jnp.zeros((tok_count, tenants), I32)
    for t in range(tok_count):
        who = jnp.where(row == t, tenant_ref[t], who)
    hot = jnp.where(lax.broadcasted_iota(I32, (tok_count, tenants), 1) == who, 1.0, 0.0)
    pages = lax.dot_general(
        hot.astype(BF),
        lookup_ref[...].astype(F32).astype(BF),
        (((1,), (1,)), ((), ())),
        preferred_element_type=F32,
    )
    pick = jnp.where(
        lax.broadcasted_iota(I32, (experts, slots), 0)
        == (lax.broadcasted_iota(I32, (experts, slots), 1) // cap) ^ mine,
        1.0,
        0.0,
    )
    page = place * jnp.dot(pages.astype(BF), pick.astype(BF), preferred_element_type=F32)
    by_token = (((0,), (0,)), ((), ()))
    rows = lax.dot_general(place.astype(BF), tok_ref[...], by_token, preferred_element_type=F32)
    tail = lax.dot_general(
        page.astype(BF), jnp.ones((tok_count, TAIL), BF), by_token, preferred_element_type=F32
    )
    for r in range(experts):
        ref = send_ref if r % 2 else keep_ref
        at = slice(r * cap, (r + 1) * cap)
        ref[r // 2, :, :width] = rows[at].astype(BF)
        ref[r // 2, :, width:] = tail[at].astype(BF)


def rows_of(own_ref, came_ref, width):
    return jnp.concatenate([own_ref[:, :width], came_ref[:, :width]], axis=0)


def shrink_kernel(n_dp, rank, own_ref, came_ref, shrink_ref, out_ref):
    wide, width = shrink_ref.shape
    col = lax.axis_index("dp")
    x = rows_of(own_ref, came_ref, width)
    page = jnp.concatenate([own_ref[:, width:], came_ref[:, width:]], axis=0).astype(F32)[:, :1]
    prod = lax.dot_general(
        x, shrink_ref[...], (((1,), (1,)), ((), ())), preferred_element_type=F32
    )
    page_of = col * (wide // rank) + lax.broadcasted_iota(I32, prod.shape, 1) // rank
    masked = jnp.where(page == page_of.astype(F32), prod, 0.0)
    out_ref[...] = turned(masked, col, n_dp, gather_order(n_dp), list(range(n_dp))).astype(BF)


def expert_kernel(n_dp, own_ref, came_ref, gate_ref, up_ref, out_ref):
    width, hid = gate_ref.shape
    col = lax.axis_index("dp")
    x = rows_of(own_ref, came_ref, width)
    gate = jnp.dot(x, gate_ref[...], preferred_element_type=F32)
    up = jnp.dot(x, up_ref[...], preferred_element_type=F32)
    act = gate / (1.0 + jnp.exp(-gate))
    for i, y in enumerate((act, act * up)):
        y = turned(y, col, n_dp, gather_order(n_dp), list(range(n_dp)))
        out_ref[:, i * hid : (i + 1) * hid] = y.astype(BF)


def grow_kernel(n_dp, low_ref, low2_ref, expand_ref, expand2_ref, act_ref, out_ref):
    here = lax.axis_index("dp") & 1
    width = act_ref.shape[1]
    hid = width // 2
    out_ref[:, :width] = act_ref[...]
    for i in range(n_dp // 2):
        at = pl.ds(pl.multiple_of((2 * i + here) * hid, hid), hid)
        part = jnp.dot(low_ref[...], expand_ref[:, at], preferred_element_type=F32)
        part += jnp.dot(low2_ref[...], expand2_ref[:, at], preferred_element_type=F32)
        out_ref[:, width + i * hid : width + (i + 1) * hid] = part.astype(BF)


def down_kernel(n_dp, hid, own_ref, came_ref, down_ref, down2_ref, keep_ref, send_ref, add_ref):
    col = lax.axis_index("dp")
    order = gather_order(n_dp)
    half = n_dp // 2
    each = half // 2
    split = 2 * hid * each
    rows = own_ref.shape[0]
    part = down_ref.shape[1]
    add_ref[...] = own_ref[:, split:].astype(F32) + came_ref[:, split:].astype(F32)
    totals = [jnp.zeros((2 * rows, part), F32)] * 2
    for i, p in enumerate(order[:half]):
        ref = own_ref if i < each else came_ref
        at = (i % each) * 2 * hid
        unit = p ^ col
        spot = pl.multiple_of((unit // 2) * hid, hid)
        start = pl.multiple_of(unit * hid, hid)
        act = ref[:, at : at + hid]
        first = ref[:, at + hid : at + 2 * hid]
        second = (act.astype(F32) * add_ref[:, pl.ds(spot, hid)]).astype(BF)
        both = jnp.concatenate([first, second], axis=0)
        for k, weight in enumerate((down_ref, down2_ref)):
            totals[k] += jnp.dot(both, weight[pl.ds(start, hid), :], preferred_element_type=F32)
    for k in range(2):
        out = totals[k][:rows] + totals[k][rows:]
        out = turned(out, col, n_dp, list(range(n_dp)), order)
        keep_ref[:, k * part : (k + 1) * part] = out[: rows // 2]
        send_ref[:, (1 - k) * part : (2 - k) * part] = out[rows // 2 :].astype(BF)


def mix_kernel(n_dp, part, mix_ref, kept_ref, came_ref, out_ref):
    col = lax.axis_index("dp")
    mix = mix_ref[...]
    blocks, cap = kept_ref.shape[:2]
    for p in range(n_dp):
        lanes = slice(p * part, (p + 1) * part)
        total = jnp.zeros((mix.shape[0], part), F32)
        for i, ref in enumerate((kept_ref, came_ref)):
            for r in range(blocks):
                x = ref[r, :, lanes].astype(F32)
                for c in range(cap):
                    at = (i * blocks + r) * cap + c
                    total += mix[:, at : at + 1] * x[c : c + 1]
        out_ref[:, pl.ds(pl.multiple_of((p ^ col) * part, part), part)] = total.astype(BF)


def hold_kernel(x_ref, *refs):
    refs[-1][...] = x_ref[...]


def hold(x, *arrays):
    return call(
        hold_kernel,
        jax.ShapeDtypeStruct(x.shape, x.dtype),
        0,
        in_specs=[VM] + [HB] * len(arrays),
    )(x, *arrays)


def call(kernel, out_shape, n_in, limit=4 << 20, **kw):
    specs = kw.pop("in_specs", [VM] * n_in)
    outs = jax.tree.map(lambda _: VM, out_shape)
    return pl.pallas_call(
        kernel,
        out_shape=out_shape,
        in_specs=specs,
        out_specs=outs,
        compiler_params=pltpu.CompilerParams(vmem_limit_bytes=limit),
        **kw,
    )


def build(mesh):
    n_exp, n_dp = mesh.shape["expert"], mesh.shape["dp"]

    def stage(blocks, axis, size, mask, dim, early=()):
        labels = sorted(blocks)
        sent = [q for q in labels if q & mask]
        x = jnp.concatenate([blocks[q] for q in sent], axis=dim)
        came = jnp.split(swap(x, axis, size, mask), len(sent), axis=dim)
        if early:
            stay = [q for q in labels if not q & mask]
            x = hold(jnp.concatenate([blocks[q] for q in stay], axis=dim), *early)
            blocks = {**blocks, **dict(zip(stay, jnp.split(x, len(stay), axis=dim)))}
        return {**blocks, **dict(zip(sent, came))}

    def per_device(
        tokens,
        routing,
        gate_quantized,
        tenant,
        tenant_page_lookup,
        gate_weight,
        up_projection,
        down_weight,
        adapter_shrink,
        adapter_expand,
    ):
        tok_count, width = tokens.shape
        experts = tenant_page_lookup.shape[0]
        cap = tok_count // 4
        pages, rank = adapter_shrink.shape[1:3]
        hid = gate_weight.shape[2]
        hidden_all = adapter_expand.shape[3]
        part = down_weight.shape[2]
        block = experts * cap
        rows = n_dp * block
        half = n_dp // 2
        shape = jax.ShapeDtypeStruct
        middle = n_exp // 2
        kept, sent, mix = call(
            slot_kernel,
            (shape((middle, cap, width + TAIL), BF),) * 2 + (shape((tok_count, block), F32),),
            5,
            limit=None,
            in_specs=[VM, VM, VM, pl.BlockSpec(memory_space=pltpu.SMEM), VM],
        )(tokens, routing, gate_quantized, tenant, tenant_page_lookup)

        state = {}
        for i in range(middle):
            state[2 * i], state[2 * i + 1] = kept[i : i + 1], sent[i : i + 1]
        gate_w = gate_weight.reshape(width, hid)
        up_w = up_projection.reshape(width, hid)
        shrink_w = adapter_shrink.reshape(pages * rank, width)
        expand_w = adapter_expand.reshape(pages * rank, hidden_all)
        down_w = down_weight.reshape(-1, part)
        expand2 = swap(expand_w, "dp", n_dp, 1)
        down2 = swap(down_w, "dp", n_dp, 1)
        plan = [(), (expand2, down2), (gate_w, up_w), (gate_w, up_w, shrink_w, expand_w)]
        early = plan[:2]
        for mask in bits_of(n_exp):
            state = stage(state, "expert", n_exp, mask, 0, early.pop(0) if early else ())
        own = jnp.concatenate([state[r] for r in range(n_exp)], axis=0)
        own = own.reshape(block, width + TAIL)
        masks = list(reversed(bits_of(n_dp)))
        for mask in masks[:-1]:
            other = swap(own, "dp", n_dp, mask)
            own = jnp.concatenate([hold(own, *plan[2]), other], axis=0)
        came = swap(own, "dp", n_dp, masks[-1])
        if plan[3]:
            own = hold(own, *plan[3])
        low = call(
            lambda *refs: shrink_kernel(n_dp, rank, *refs), shape((rows, pages * rank), BF), 3
        )(own, came, shrink_w)
        low2 = swap(low, "dp", n_dp, 1)
        acts = call(
            lambda *refs: expert_kernel(n_dp, *refs),
            shape((rows, 2 * hid), BF),
            4,
            cost_estimate=pl.CostEstimate(
                flops=4 * rows * width * hid, bytes_accessed=4 * width * hid, transcendentals=0
            ),
        )(own, came, gate_w, up_w)
        packed = call(
            lambda *refs: grow_kernel(n_dp, *refs), shape((rows, 2 * hid + hidden_all // 2), BF), 5
        )(low, low2, expand_w, expand2, acts)

        for mask in masks[:-2]:
            other = swap(packed, "dp", n_dp, mask)
            at = packed.shape[1] - hidden_all // 2
            packed = jnp.concatenate(
                [packed[:, :at], other[:, :at], packed[:, at:] + other[:, at:]], axis=1
            )
        other = swap(packed, "dp", n_dp, masks[-2])
        keep, send = call(
            lambda *refs: down_kernel(n_dp, hid, *refs),
            (shape((rows // 2, 2 * part), F32), shape((rows // 2, 2 * part), BF)),
            4,
            scratch_shapes=[pltpu.VMEM((rows, hidden_all // 2), F32)],
        )(packed, other, down_w, down2)

        back = swap(send, "dp", n_dp, 1)
        both = (keep + back.astype(F32)).astype(BF)
        order = gather_order(n_dp)[:half]
        state = {q: both[i * block : (i + 1) * block] for i, q in enumerate(order)}
        for mask in bits_of(n_dp)[1:]:
            state = stage(state, "dp", n_dp, mask, 0)
        home = jnp.concatenate([state[q] for q in sorted(state)], axis=1)
        home = home.reshape(n_exp, cap, n_dp * part)
        state = {r: home[r : r + 1] for r in range(n_exp)}
        for mask in bits_of(n_exp)[:-1]:
            state = stage(state, "expert", n_exp, mask, 0)
        kept = jnp.concatenate([state[r] for r in range(middle)], axis=0)
        sent = jnp.concatenate([state[r] for r in range(middle, n_exp)], axis=0)
        came = swap(sent, "expert", n_exp, middle)
        return call(
            lambda *refs: mix_kernel(n_dp, part, *refs),
            shape((tok_count, n_dp * part), BF),
            3,
        )(mix, kept, came)

    return per_device


def solution(mesh):
    row = ("group", "expert", "dp")
    return jax.shard_map(
        build(mesh),
        mesh=mesh,
        in_specs=(
            P(row, None),
            P(row, None),
            P(row, None),
            P(row),
            P(),
            P("expert", None, "dp"),
            P("expert", None, "dp"),
            P("expert", None, "dp"),
            P("expert", "dp", None, None),
            P("expert", "dp", None, None),
        ),
        out_specs=P(row, None),
        check_vma=False,
    )
```

```python
import jax
import jax.numpy as jnp
from jax import lax
from jax.experimental import pallas as pl
from jax.experimental.pallas import tpu as pltpu
from jax.sharding import PartitionSpec as P

BF = jnp.bfloat16
F32 = jnp.float32
I32 = jnp.int32
TAIL = 128
VM = pl.BlockSpec(memory_space=pltpu.VMEM)
HB = pl.BlockSpec(memory_space=pl.ANY)


def swap(x, axis, size, mask):
    return lax.ppermute(x, axis, [(i, i ^ mask) for i in range(size)])


def bits_of(size):
    return [1 << b for b in range(size.bit_length() - 1)]


def gather_order(size):
    order = [0]
    for mask in reversed(bits_of(size)):
        order = order + [q ^ mask for q in order]
    return order


def turned(x, col, size, names_in, names_out):
    rows = x.shape[0] // size
    block = {q: x[i * rows : (i + 1) * rows] for i, q in enumerate(names_in)}
    for mask in bits_of(size):
        here = (col & mask) != 0
        block = {q: jnp.where(here, block[q ^ mask], block[q]) for q in range(size)}
    return jnp.concatenate([block[q] for q in names_out], axis=0)


def slot_kernel(
    tok_ref, routing_ref, gate_ref, tenant_ref, lookup_ref, keep_ref, send_ref, mix_ref
):
    tok_count, width = tok_ref.shape
    experts, tenants = lookup_ref.shape
    slots = mix_ref.shape[1]
    cap = slots // experts
    topk = routing_ref.shape[1]
    mine = lax.axis_index("expert")
    lane = lax.broadcasted_iota(I32, (tok_count, slots), 1)
    expert_of = (lane // cap) ^ mine
    routing = routing_ref[...]
    quant = gate_ref[...].astype(F32) * (1.0 / 32768.0)
    assign = jnp.zeros((tok_count, slots), F32)
    coef = jnp.zeros((tok_count, slots), F32)
    for k in range(topk):
        match = routing[:, k : k + 1] == expert_of
        assign = jnp.where(match, 1.0, assign)
        coef = jnp.where(match, quant[:, k : k + 1], coef)
    below = lax.broadcasted_iota(I32, (tok_count, tok_count), 0) > lax.broadcasted_iota(
        I32, (tok_count, tok_count), 1
    )
    slot_rank = jnp.dot(
        jnp.where(below, 1.0, 0.0).astype(BF), assign.astype(BF), preferred_element_type=F32
    )
    place = jnp.where(slot_rank == (lane % cap).astype(F32), assign, 0.0)
    mix_ref[...] = place * coef
    row = lax.broadcasted_iota(I32, (tok_count, tenants), 0)
    who = jnp.zeros((tok_count, tenants), I32)
    for t in range(tok_count):
        who = jnp.where(row == t, tenant_ref[t], who)
    hot = jnp.where(lax.broadcasted_iota(I32, (tok_count, tenants), 1) == who, 1.0, 0.0)
    pages = lax.dot_general(
        hot.astype(BF),
        lookup_ref[...].astype(F32).astype(BF),
        (((1,), (1,)), ((), ())),
        preferred_element_type=F32,
    )
    pick = jnp.where(
        lax.broadcasted_iota(I32, (experts, slots), 0)
        == (lax.broadcasted_iota(I32, (experts, slots), 1) // cap) ^ mine,
        1.0,
        0.0,
    )
    page = place * jnp.dot(pages.astype(BF), pick.astype(BF), preferred_element_type=F32)
    by_token = (((0,), (0,)), ((), ()))
    rows = lax.dot_general(place.astype(BF), tok_ref[...], by_token, preferred_element_type=F32)
    tail = lax.dot_general(
        page.astype(BF), jnp.ones((tok_count, TAIL), BF), by_token, preferred_element_type=F32
    )
    for r in range(experts):
        ref = send_ref if r % 2 else keep_ref
        at = slice(r * cap, (r + 1) * cap)
        ref[r // 2, :, :width] = rows[at].astype(BF)
        ref[r // 2, :, width:] = tail[at].astype(BF)


def rows_of(own_ref, came_ref, width):
    return jnp.concatenate([own_ref[:, :width], came_ref[:, :width]], axis=0)


def shrink_kernel(n_dp, rank, own_ref, came_ref, shrink_ref, out_ref):
    wide, width = shrink_ref.shape
    col = lax.axis_index("dp")
    x = rows_of(own_ref, came_ref, width)
    page = jnp.concatenate([own_ref[:, width:], came_ref[:, width:]], axis=0).astype(F32)[:, :1]
    prod = lax.dot_general(
        x, shrink_ref[...], (((1,), (1,)), ((), ())), preferred_element_type=F32
    )
    page_of = col * (wide // rank) + lax.broadcasted_iota(I32, prod.shape, 1) // rank
    masked = jnp.where(page == page_of.astype(F32), prod, 0.0)
    out_ref[...] = turned(masked, col, n_dp, gather_order(n_dp), list(range(n_dp))).astype(BF)


def expert_kernel(n_dp, own_ref, came_ref, gate_ref, up_ref, out_ref):
    width, hid = gate_ref.shape
    col = lax.axis_index("dp")
    x = rows_of(own_ref, came_ref, width)
    gate = jnp.dot(x, gate_ref[...], preferred_element_type=F32)
    up = jnp.dot(x, up_ref[...], preferred_element_type=F32)
    act = gate / (1.0 + jnp.exp(-gate))
    for i, y in enumerate((act, up)):
        y = turned(y, col, n_dp, gather_order(n_dp), list(range(n_dp)))
        out_ref[:, i * hid : (i + 1) * hid] = y


def grow_kernel(n_dp, low_ref, low2_ref, expand_ref, expand2_ref, act_ref, out_ref):
    col = lax.axis_index("dp")
    hid = act_ref.shape[1] // 2
    half = n_dp // 2

    def update(unit):
        at = pl.ds(pl.multiple_of(unit * hid, hid), hid)
        y = jnp.dot(low_ref[...], expand_ref[:, at], preferred_element_type=F32)
        return y + jnp.dot(low2_ref[...], expand2_ref[:, at], preferred_element_type=F32)

    act = act_ref[:, :hid]
    out_ref[:, :hid] = act.astype(BF)
    out_ref[:, hid : 2 * hid] = (act * (act_ref[:, hid:] + update(col))).astype(BF)
    if half == 2:
        out_ref[:, 2 * hid :] = update(col ^ 2).astype(BF)
    else:
        for i in range(half):
            unit = 2 * i + (col & 1)
            y = jnp.where(unit == col, 0.0, update(unit))
            out_ref[:, (2 + i) * hid : (3 + i) * hid] = y.astype(BF)


def down_kernel(n_dp, hid, own_ref, came_ref, down_ref, down2_ref, keep_ref, send_ref):
    col = lax.axis_index("dp")
    order = gather_order(n_dp)
    half = n_dp // 2
    each = half // 2
    split = 2 * hid * each
    rows = own_ref.shape[0]
    part = down_ref.shape[1]
    totals = [jnp.zeros((2 * rows, part), F32)] * 2
    for i, p in enumerate(order[:half]):
        ref, other = (own_ref, came_ref) if i < each else (came_ref, own_ref)
        at = (i % each) * 2 * hid
        unit = p ^ col
        start = pl.multiple_of(unit * hid, hid)
        if half == 2:
            add = other[:, split:].astype(F32)
        else:
            spot = pl.ds(pl.multiple_of(split + (unit // 2) * hid, hid), hid)
            add = ref[:, spot].astype(F32) + other[:, spot].astype(F32)
        first = ref[:, at + hid : at + 2 * hid]
        second = (ref[:, at : at + hid].astype(F32) * add).astype(BF)
        both = jnp.concatenate([first, second], axis=0)
        for k, weight in enumerate((down_ref, down2_ref)):
            totals[k] += jnp.dot(both, weight[pl.ds(start, hid), :], preferred_element_type=F32)
    for k in range(2):
        out = totals[k][:rows] + totals[k][rows:]
        out = turned(out, col, n_dp, list(range(n_dp)), order)
        keep_ref[:, k * part : (k + 1) * part] = out[: rows // 2]
        send_ref[:, (1 - k) * part : (2 - k) * part] = out[rows // 2 :].astype(BF)


def mix_kernel(n_dp, part, mix_ref, kept_ref, came_ref, out_ref):
    col = lax.axis_index("dp")
    mix = mix_ref[...]
    blocks, cap = kept_ref.shape[:2]
    for p in range(n_dp):
        lanes = slice(p * part, (p + 1) * part)
        total = jnp.zeros((mix.shape[0], part), F32)
        for i, ref in enumerate((kept_ref, came_ref)):
            for r in range(blocks):
                x = ref[r, :, lanes].astype(F32)
                for c in range(cap):
                    at = (i * blocks + r) * cap + c
                    total += mix[:, at : at + 1] * x[c : c + 1]
        out_ref[:, pl.ds(pl.multiple_of((p ^ col) * part, part), part)] = total.astype(BF)


def hold_kernel(x_ref, *refs):
    refs[-1][...] = x_ref[...]


def hold(x, *arrays):
    return call(
        hold_kernel,
        jax.ShapeDtypeStruct(x.shape, x.dtype),
        0,
        in_specs=[VM] + [HB] * len(arrays),
    )(x, *arrays)


def call(kernel, out_shape, n_in, limit=4 << 20, **kw):
    specs = kw.pop("in_specs", [VM] * n_in)
    outs = jax.tree.map(lambda _: VM, out_shape)
    return pl.pallas_call(
        kernel,
        out_shape=out_shape,
        in_specs=specs,
        out_specs=outs,
        compiler_params=pltpu.CompilerParams(vmem_limit_bytes=limit),
        **kw,
    )


def build(mesh):
    n_exp, n_dp = mesh.shape["expert"], mesh.shape["dp"]

    def stage(blocks, axis, size, mask, dim, early=()):
        labels = sorted(blocks)
        sent = [q for q in labels if q & mask]
        x = jnp.concatenate([blocks[q] for q in sent], axis=dim)
        came = jnp.split(swap(x, axis, size, mask), len(sent), axis=dim)
        if early:
            stay = [q for q in labels if not q & mask]
            x = hold(jnp.concatenate([blocks[q] for q in stay], axis=dim), *early)
            blocks = {**blocks, **dict(zip(stay, jnp.split(x, len(stay), axis=dim)))}
        return {**blocks, **dict(zip(sent, came))}

    def per_device(
        tokens,
        routing,
        gate_quantized,
        tenant,
        tenant_page_lookup,
        gate_weight,
        up_projection,
        down_weight,
        adapter_shrink,
        adapter_expand,
    ):
        tok_count, width = tokens.shape
        experts = tenant_page_lookup.shape[0]
        cap = tok_count // 4
        pages, rank = adapter_shrink.shape[1:3]
        hid = gate_weight.shape[2]
        hidden_all = adapter_expand.shape[3]
        part = down_weight.shape[2]
        block = experts * cap
        rows = n_dp * block
        half = n_dp // 2
        shape = jax.ShapeDtypeStruct
        middle = n_exp // 2
        kept, sent, mix = call(
            slot_kernel,
            (shape((middle, cap, width + TAIL), BF),) * 2 + (shape((tok_count, block), F32),),
            5,
            limit=None,
            in_specs=[VM, VM, VM, pl.BlockSpec(memory_space=pltpu.SMEM), VM],
        )(tokens, routing, gate_quantized, tenant, tenant_page_lookup)

        state = {}
        for i in range(middle):
            state[2 * i], state[2 * i + 1] = kept[i : i + 1], sent[i : i + 1]
        gate_w = gate_weight.reshape(width, hid)
        up_w = up_projection.reshape(width, hid)
        shrink_w = adapter_shrink.reshape(pages * rank, width)
        expand_w = adapter_expand.reshape(pages * rank, hidden_all)
        down_w = down_weight.reshape(-1, part)
        expand2 = swap(expand_w, "dp", n_dp, 1)
        down2 = swap(down_w, "dp", n_dp, 1)
        plan = [(), (expand2, down2), (gate_w, up_w), (gate_w, up_w, shrink_w, expand_w)]
        early = plan[:2]
        for mask in bits_of(n_exp):
            state = stage(state, "expert", n_exp, mask, 0, early.pop(0) if early else ())
        own = jnp.concatenate([state[r] for r in range(n_exp)], axis=0)
        own = own.reshape(block, width + TAIL)
        masks = list(reversed(bits_of(n_dp)))
        for mask in masks[:-1]:
            other = swap(own, "dp", n_dp, mask)
            own = jnp.concatenate([hold(own, *plan[2]), other], axis=0)
        came = swap(own, "dp", n_dp, masks[-1])
        if plan[3]:
            own = hold(own, *plan[3])
        low = call(
            lambda *refs: shrink_kernel(n_dp, rank, *refs), shape((rows, pages * rank), BF), 3
        )(own, came, shrink_w)
        low2 = swap(low, "dp", n_dp, 1)
        acts = call(
            lambda *refs: expert_kernel(n_dp, *refs),
            shape((rows, 2 * hid), F32),
            4,
            cost_estimate=pl.CostEstimate(
                flops=4 * rows * width * hid, bytes_accessed=4 * width * hid, transcendentals=0
            ),
        )(own, came, gate_w, up_w)
        split = 2 * hid
        parts = 1 if half == 2 else half
        packed = call(
            lambda *refs: grow_kernel(n_dp, *refs), shape((rows, split + parts * hid), BF), 5
        )(low, low2, expand_w, expand2, acts)

        for mask in masks[:-2]:
            other = swap(packed, "dp", n_dp, mask)
            at = packed.shape[1] - parts * hid
            packed = jnp.concatenate(
                [packed[:, :at], other[:, :at], packed[:, at:] + other[:, at:]], axis=1
            )
        other = swap(packed, "dp", n_dp, masks[-2])
        keep, send = call(
            lambda *refs: down_kernel(n_dp, hid, *refs),
            (shape((rows // 2, 2 * part), F32), shape((rows // 2, 2 * part), BF)),
            4,
        )(packed, other, down_w, down2)

        back = swap(send, "dp", n_dp, 1)
        both = (keep + back.astype(F32)).astype(BF)
        order = gather_order(n_dp)[:half]
        state = {q: both[i * block : (i + 1) * block] for i, q in enumerate(order)}
        for mask in bits_of(n_dp)[1:]:
            state = stage(state, "dp", n_dp, mask, 0)
        home = jnp.concatenate([state[q] for q in sorted(state)], axis=1)
        home = home.reshape(n_exp, cap, n_dp * part)
        state = {r: home[r : r + 1] for r in range(n_exp)}
        for mask in bits_of(n_exp)[:-1]:
            state = stage(state, "expert", n_exp, mask, 0)
        kept = jnp.concatenate([state[r] for r in range(middle)], axis=0)
        sent = jnp.concatenate([state[r] for r in range(middle, n_exp)], axis=0)
        came = swap(sent, "expert", n_exp, middle)
        return call(
            lambda *refs: mix_kernel(n_dp, part, *refs),
            shape((tok_count, n_dp * part), BF),
            3,
        )(mix, kept, came)

    return per_device


def solution(mesh):
    row = ("group", "expert", "dp")
    return jax.shard_map(
        build(mesh),
        mesh=mesh,
        in_specs=(
            P(row, None),
            P(row, None),
            P(row, None),
            P(row),
            P(),
            P("expert", None, "dp"),
            P("expert", None, "dp"),
            P("expert", None, "dp"),
            P("expert", "dp", None, None),
            P("expert", "dp", None, None),
        ),
        out_specs=P(row, None),
        check_vma=False,
    )
```

```python
import jax
import jax.numpy as jnp
from jax import lax
from jax.experimental import pallas as pl
from jax.experimental.pallas import tpu as pltpu
from jax.sharding import PartitionSpec as P

BF = jnp.bfloat16
F32 = jnp.float32
I32 = jnp.int32
TAIL = 128
VM = pl.BlockSpec(memory_space=pltpu.VMEM)
HB = pl.BlockSpec(memory_space=pl.ANY)


def swap(x, axis, size, mask):
    return lax.ppermute(x, axis, [(i, i ^ mask) for i in range(size)])


def bits_of(size):
    return [1 << b for b in range(size.bit_length() - 1)]


def gather_order(size):
    order = [0]
    for mask in bits_of(size)[1:] + [1]:
        order = order + [q ^ mask for q in order]
    return order


def turned(x, col, size, names_in, names_out):
    rows = x.shape[0] // size
    block = {q: x[i * rows : (i + 1) * rows] for i, q in enumerate(names_in)}
    for mask in bits_of(size):
        here = (col & mask) != 0
        block = {q: jnp.where(here, block[q ^ mask], block[q]) for q in range(size)}
    return jnp.concatenate([block[q] for q in names_out], axis=0)


def slot_kernel(
    tok_ref, routing_ref, gate_ref, tenant_ref, lookup_ref, keep_ref, send_ref, mix_ref
):
    tok_count, width = tok_ref.shape
    experts, tenants = lookup_ref.shape
    slots = mix_ref.shape[1]
    cap = slots // experts
    topk = routing_ref.shape[1]
    mine = lax.axis_index("expert")
    lane = lax.broadcasted_iota(I32, (tok_count, slots), 1)
    expert_of = (lane // cap) ^ mine
    routing = routing_ref[...]
    quant = gate_ref[...].astype(F32) * (1.0 / 32768.0)
    assign = jnp.zeros((tok_count, slots), F32)
    coef = jnp.zeros((tok_count, slots), F32)
    for k in range(topk):
        match = routing[:, k : k + 1] == expert_of
        assign = jnp.where(match, 1.0, assign)
        coef = jnp.where(match, quant[:, k : k + 1], coef)
    below = lax.broadcasted_iota(I32, (tok_count, tok_count), 0) > lax.broadcasted_iota(
        I32, (tok_count, tok_count), 1
    )
    slot_rank = jnp.dot(
        jnp.where(below, 1.0, 0.0).astype(BF), assign.astype(BF), preferred_element_type=F32
    )
    place = jnp.where(slot_rank == (lane % cap).astype(F32), assign, 0.0)
    mix_ref[...] = place * coef
    row = lax.broadcasted_iota(I32, (tok_count, tenants), 0)
    who = jnp.zeros((tok_count, tenants), I32)
    for t in range(tok_count):
        who = jnp.where(row == t, tenant_ref[t], who)
    hot = jnp.where(lax.broadcasted_iota(I32, (tok_count, tenants), 1) == who, 1.0, 0.0)
    pages = lax.dot_general(
        hot.astype(BF),
        lookup_ref[...].astype(F32).astype(BF),
        (((1,), (1,)), ((), ())),
        preferred_element_type=F32,
    )
    pick = jnp.where(
        lax.broadcasted_iota(I32, (experts, slots), 0)
        == (lax.broadcasted_iota(I32, (experts, slots), 1) // cap) ^ mine,
        1.0,
        0.0,
    )
    page = place * jnp.dot(pages.astype(BF), pick.astype(BF), preferred_element_type=F32)
    by_token = (((0,), (0,)), ((), ()))
    rows = lax.dot_general(place.astype(BF), tok_ref[...], by_token, preferred_element_type=F32)
    tail = lax.dot_general(
        page.astype(BF), jnp.ones((tok_count, TAIL), BF), by_token, preferred_element_type=F32
    )
    for r in range(experts):
        middle = experts // 2
        ref = send_ref if r >= middle else keep_ref
        at = slice(r * cap, (r + 1) * cap)
        ref[r % middle, :, :width] = rows[at].astype(BF)
        ref[r % middle, :, width:] = tail[at].astype(BF)


def rows_of(own_ref, came_ref, width):
    return jnp.concatenate([own_ref[:, :width], came_ref[:, :width]], axis=0)


def shrink_kernel(n_dp, rank, own_ref, came_ref, shrink_ref, out_ref):
    wide, width = shrink_ref.shape
    col = lax.axis_index("dp")
    x = rows_of(own_ref, came_ref, width)
    page = jnp.concatenate([own_ref[:, width:], came_ref[:, width:]], axis=0).astype(F32)[:, :1]
    prod = lax.dot_general(
        x, shrink_ref[...], (((1,), (1,)), ((), ())), preferred_element_type=F32
    )
    page_of = col * (wide // rank) + lax.broadcasted_iota(I32, prod.shape, 1) // rank
    masked = jnp.where(page == page_of.astype(F32), prod, 0.0)
    out_ref[...] = turned(masked, col, n_dp, gather_order(n_dp), list(range(n_dp))).astype(BF)


def expert_kernel(n_dp, own_ref, came_ref, gate_ref, up_ref, out_ref):
    width, hid = gate_ref.shape
    col = lax.axis_index("dp")
    x = rows_of(own_ref, came_ref, width)
    gate = jnp.dot(x, gate_ref[...], preferred_element_type=F32)
    up = jnp.dot(x, up_ref[...], preferred_element_type=F32)
    act = gate / (1.0 + jnp.exp(-gate))
    for i, y in enumerate((act, up)):
        y = turned(y, col, n_dp, gather_order(n_dp), list(range(n_dp)))
        out_ref[:, i * hid : (i + 1) * hid] = y


def grow_kernel(n_dp, low_ref, low2_ref, expand_ref, expand2_ref, act_ref, out_ref):
    col = lax.axis_index("dp")
    hid = act_ref.shape[1] // 2
    half = n_dp // 2

    def update(unit):
        at = pl.ds(pl.multiple_of(unit * hid, hid), hid)
        y = jnp.dot(low_ref[...], expand_ref[:, at], preferred_element_type=F32)
        return y + jnp.dot(low2_ref[...], expand2_ref[:, at], preferred_element_type=F32)

    act = act_ref[:, :hid]
    out_ref[:, :hid] = act.astype(BF)
    out_ref[:, hid : 2 * hid] = (act * (act_ref[:, hid:] + update(col))).astype(BF)
    if half == 2:
        out_ref[:, 2 * hid :] = update(col ^ 2).astype(BF)
    else:
        for i in range(half):
            unit = 2 * i + (col & 1)
            y = jnp.where(unit == col, 0.0, update(unit))
            out_ref[:, (2 + i) * hid : (3 + i) * hid] = y.astype(BF)


def down_kernel(n_dp, hid, own_ref, came_ref, down_ref, down2_ref, keep_ref, send_ref):
    col = lax.axis_index("dp")
    order = gather_order(n_dp)
    half = n_dp // 2
    each = half // 2
    split = 2 * hid * each
    rows = own_ref.shape[0]
    part = down_ref.shape[1]
    totals = [jnp.zeros((2 * rows, part), F32)] * 2
    for i, p in enumerate(order[:half]):
        ref, other = (own_ref, came_ref) if i < each else (came_ref, own_ref)
        at = (i % each) * 2 * hid
        unit = p ^ col
        start = pl.multiple_of(unit * hid, hid)
        if half == 2:
            add = other[:, split:].astype(F32)
        else:
            spot = pl.ds(pl.multiple_of(split + (unit // 2) * hid, hid), hid)
            add = ref[:, spot].astype(F32) + other[:, spot].astype(F32)
        first = ref[:, at + hid : at + 2 * hid]
        second = (ref[:, at : at + hid].astype(F32) * add).astype(BF)
        both = jnp.concatenate([first, second], axis=0)
        for k, weight in enumerate((down_ref, down2_ref)):
            totals[k] += jnp.dot(both, weight[pl.ds(start, hid), :], preferred_element_type=F32)
    for k in range(2):
        out = totals[k][:rows] + totals[k][rows:]
        out = turned(out, col, n_dp, list(range(n_dp)), order)
        keep_ref[:, k * part : (k + 1) * part] = out[: rows // 2]
        send_ref[:, (1 - k) * part : (2 - k) * part] = out[rows // 2 :].astype(BF)


def mix_kernel(n_dp, part, mix_ref, kept_ref, came_ref, out_ref):
    col = lax.axis_index("dp")
    mix = mix_ref[...]
    blocks, cap = kept_ref.shape[:2]
    for p in range(n_dp):
        lanes = slice(p * part, (p + 1) * part)
        total = jnp.zeros((mix.shape[0], part), F32)
        for i, ref in enumerate((kept_ref, came_ref)):
            for r in range(blocks):
                x = ref[r, :, lanes].astype(F32)
                for c in range(cap):
                    at = (i * blocks + r) * cap + c
                    total += mix[:, at : at + 1] * x[c : c + 1]
        out_ref[:, pl.ds(pl.multiple_of((p ^ col) * part, part), part)] = total.astype(BF)


def hold_kernel(x_ref, *refs):
    refs[-1][...] = x_ref[...]


def hold(x, *arrays):
    return call(
        hold_kernel,
        jax.ShapeDtypeStruct(x.shape, x.dtype),
        0,
        in_specs=[VM] + [HB] * len(arrays),
    )(x, *arrays)


def call(kernel, out_shape, n_in, limit=4 << 20, **kw):
    specs = kw.pop("in_specs", [VM] * n_in)
    outs = jax.tree.map(lambda _: VM, out_shape)
    return pl.pallas_call(
        kernel,
        out_shape=out_shape,
        in_specs=specs,
        out_specs=outs,
        compiler_params=pltpu.CompilerParams(vmem_limit_bytes=limit),
        **kw,
    )


def build(mesh):
    n_exp, n_dp = mesh.shape["expert"], mesh.shape["dp"]

    n_all = n_exp * n_dp
    both_axes = ("expert", "dp")

    def stage(blocks, axis, size, mask, dim):
        sent = [q for q in sorted(blocks) if q & mask]
        x = jnp.concatenate([blocks[q] for q in sent], axis=dim)
        came = jnp.split(swap(x, axis, size, mask), len(sent), axis=dim)
        return {**blocks, **dict(zip(sent, came))}

    def per_device(
        tokens,
        routing,
        gate_quantized,
        tenant,
        tenant_page_lookup,
        gate_weight,
        up_projection,
        down_weight,
        adapter_shrink,
        adapter_expand,
    ):
        tok_count, width = tokens.shape
        experts = tenant_page_lookup.shape[0]
        cap = tok_count // 4
        pages, rank = adapter_shrink.shape[1:3]
        hid = gate_weight.shape[2]
        hidden_all = adapter_expand.shape[3]
        part = down_weight.shape[2]
        block = experts * cap
        rows = n_dp * block
        half = n_dp // 2
        shape = jax.ShapeDtypeStruct
        middle = n_exp // 2
        kept, sent, mix = call(
            slot_kernel,
            (shape((middle, cap, width + TAIL), BF),) * 2 + (shape((tok_count, block), F32),),
            5,
            limit=None,
            in_specs=[VM, VM, VM, pl.BlockSpec(memory_space=pltpu.SMEM), VM],
        )(tokens, routing, gate_quantized, tenant, tenant_page_lookup)

        state = {}
        for i in range(middle):
            state[i], state[middle + i] = kept[i : i + 1], sent[i : i + 1]
        gate_w = gate_weight.reshape(width, hid)
        up_w = up_projection.reshape(width, hid)
        shrink_w = adapter_shrink.reshape(pages * rank, width)
        expand_w = adapter_expand.reshape(pages * rank, hidden_all)
        down_w = down_weight.reshape(-1, part)
        expand2 = swap(expand_w, "dp", n_dp, 1)
        down2 = swap(down_w, "dp", n_dp, 1)
        for mask in reversed(bits_of(n_exp)[1:]):
            state = stage(state, "expert", n_exp, mask, 0)
        even = jnp.concatenate([state[r] for r in range(0, n_exp, 2)], axis=0)
        odd = jnp.concatenate([state[r] for r in range(1, n_exp, 2)], axis=0)
        beside = swap(even, "dp", n_dp, 2)
        across = swap(odd, "expert", n_exp, 1)
        corner = swap(odd, both_axes, n_all, n_dp | 2)
        even = hold(hold(even, expand2, down2), gate_w, up_w)
        own = jnp.concatenate([even, across, beside, corner], axis=0)
        own = own.reshape(2 * block, width + TAIL)
        masks = bits_of(n_dp)[1:] + [1]
        for mask in masks[1:-1]:
            own = jnp.concatenate([own, swap(own, "dp", n_dp, mask)], axis=0)
        came = swap(own, "dp", n_dp, 1)
        own = hold(own, gate_w, shrink_w, expand_w)
        low = call(
            lambda *refs: shrink_kernel(n_dp, rank, *refs), shape((rows, pages * rank), BF), 3
        )(own, came, shrink_w)
        low2 = swap(low, "dp", n_dp, 1)
        acts = call(
            lambda *refs: expert_kernel(n_dp, *refs),
            shape((rows, 2 * hid), F32),
            4,
            cost_estimate=pl.CostEstimate(
                flops=4 * rows * width * hid, bytes_accessed=4 * width * hid, transcendentals=0
            ),
        )(own, came, gate_w, up_w)
        split = 2 * hid
        parts = 1 if half == 2 else half
        packed = call(
            lambda *refs: grow_kernel(n_dp, *refs), shape((rows, split + parts * hid), BF), 5
        )(low, low2, expand_w, expand2, acts)

        for mask in masks[:-2]:
            other = swap(packed, "dp", n_dp, mask)
            at = packed.shape[1] - parts * hid
            packed = jnp.concatenate(
                [packed[:, :at], other[:, :at], packed[:, at:] + other[:, at:]], axis=1
            )
        other = swap(packed, "dp", n_dp, masks[-2])
        keep, send = call(
            lambda *refs: down_kernel(n_dp, hid, *refs),
            (shape((rows // 2, 2 * part), F32), shape((rows // 2, 2 * part), BF)),
            4,
        )(packed, other, down_w, down2)

        back = swap(send, "dp", n_dp, 1)
        both = (keep + back.astype(F32)).astype(BF)
        order = gather_order(n_dp)[:half]
        each = block // 2
        state = {}
        for i, q in enumerate(order):
            for odd in range(2):
                at = i * block + odd * each
                state[q, odd] = both[at : at + each]
        for odd, far, axis, size, mask in (
            (0, 2, "dp", n_dp, 2),
            (1, 0, "expert", n_exp, 1),
            (1, 2, both_axes, n_all, n_dp | 2),
        ):
            sent = [q for q in order if (q & 2) == far]
            came = swap(jnp.concatenate([state[q, odd] for q in sent], axis=0), axis, size, mask)
            for q, x in zip(sent, jnp.split(came, len(sent), axis=0)):
                state[q, odd] = x
        home = {q: jnp.concatenate([state[q, 0], state[q, 1]], axis=0) for q in order}
        for mask in masks[1:-1]:
            home = stage(home, "dp", n_dp, mask, 0)
        home = jnp.concatenate([home[q] for q in sorted(home)], axis=1)
        home = home.reshape(n_exp, cap, n_dp * part)
        labels = list(range(0, n_exp, 2)) + list(range(1, n_exp, 2))
        state = {r: home[i : i + 1] for i, r in enumerate(labels)}
        for mask in bits_of(n_exp)[1:-1]:
            state = stage(state, "expert", n_exp, mask, 0)
        kept = jnp.concatenate([state[r] for r in range(middle)], axis=0)
        sent = jnp.concatenate([state[r] for r in range(middle, n_exp)], axis=0)
        came = swap(sent, "expert", n_exp, middle)
        return call(
            lambda *refs: mix_kernel(n_dp, part, *refs),
            shape((tok_count, n_dp * part), BF),
            3,
        )(mix, kept, came)

    return per_device


def solution(mesh):
    row = ("group", "expert", "dp")
    return jax.shard_map(
        build(mesh),
        mesh=mesh,
        in_specs=(
            P(row, None),
            P(row, None),
            P(row, None),
            P(row),
            P(),
            P("expert", None, "dp"),
            P("expert", None, "dp"),
            P("expert", None, "dp"),
            P("expert", "dp", None, None),
            P("expert", "dp", None, None),
        ),
        out_specs=P(row, None),
        check_vma=False,
    )
```

```python
import jax
import jax.numpy as jnp
from jax import lax
from jax.experimental import pallas as pl
from jax.experimental.pallas import tpu as pltpu
from jax.sharding import PartitionSpec as P

BF = jnp.bfloat16
F32 = jnp.float32
I32 = jnp.int32
TAIL = 128
VM = pl.BlockSpec(memory_space=pltpu.VMEM)
HB = pl.BlockSpec(memory_space=pl.ANY)


def swap(x, axis, size, mask):
    return lax.ppermute(x, axis, [(i, i ^ mask) for i in range(size)])


def bits_of(size):
    return [1 << b for b in range(size.bit_length() - 1)]


def gather_order(size):
    order = [0]
    for mask in bits_of(size)[1:] + [1]:
        order = order + [q ^ mask for q in order]
    return order


def turned(x, col, size, names_in, names_out):
    rows = x.shape[0] // size
    block = {q: x[i * rows : (i + 1) * rows] for i, q in enumerate(names_in)}
    for mask in bits_of(size):
        here = (col & mask) != 0
        block = {q: jnp.where(here, block[q ^ mask], block[q]) for q in range(size)}
    return jnp.concatenate([block[q] for q in names_out], axis=0)


def slot_kernel(
    tok_ref, routing_ref, gate_ref, tenant_ref, lookup_ref, keep_ref, send_ref, mix_ref
):
    tok_count, width = tok_ref.shape
    experts, tenants = lookup_ref.shape
    slots = mix_ref.shape[1]
    cap = slots // experts
    topk = routing_ref.shape[1]
    mine = lax.axis_index("expert")
    lane = lax.broadcasted_iota(I32, (tok_count, slots), 1)
    expert_of = (lane // cap) ^ mine
    routing = routing_ref[...]
    quant = gate_ref[...].astype(F32) * (1.0 / 32768.0)
    assign = jnp.zeros((tok_count, slots), F32)
    coef = jnp.zeros((tok_count, slots), F32)
    for k in range(topk):
        match = routing[:, k : k + 1] == expert_of
        assign = jnp.where(match, 1.0, assign)
        coef = jnp.where(match, quant[:, k : k + 1], coef)
    below = lax.broadcasted_iota(I32, (tok_count, tok_count), 0) > lax.broadcasted_iota(
        I32, (tok_count, tok_count), 1
    )
    slot_rank = jnp.dot(
        jnp.where(below, 1.0, 0.0).astype(BF), assign.astype(BF), preferred_element_type=F32
    )
    place = jnp.where(slot_rank == (lane % cap).astype(F32), assign, 0.0)
    mix_ref[...] = place * coef
    row = lax.broadcasted_iota(I32, (tok_count, tenants), 0)
    who = jnp.zeros((tok_count, tenants), I32)
    for t in range(tok_count):
        who = jnp.where(row == t, tenant_ref[t], who)
    hot = jnp.where(lax.broadcasted_iota(I32, (tok_count, tenants), 1) == who, 1.0, 0.0)
    pages = lax.dot_general(
        hot.astype(BF),
        lookup_ref[...].astype(F32).astype(BF),
        (((1,), (1,)), ((), ())),
        preferred_element_type=F32,
    )
    pick = jnp.where(
        lax.broadcasted_iota(I32, (experts, slots), 0)
        == (lax.broadcasted_iota(I32, (experts, slots), 1) // cap) ^ mine,
        1.0,
        0.0,
    )
    page = place * jnp.dot(pages.astype(BF), pick.astype(BF), preferred_element_type=F32)
    by_token = (((0,), (0,)), ((), ()))
    rows = lax.dot_general(place.astype(BF), tok_ref[...], by_token, preferred_element_type=F32)
    tail = lax.dot_general(
        page.astype(BF), jnp.ones((tok_count, TAIL), BF), by_token, preferred_element_type=F32
    )
    for r in range(experts):
        middle = experts // 2
        ref = send_ref if r >= middle else keep_ref
        at = slice(r * cap, (r + 1) * cap)
        ref[r % middle, :, :width] = rows[at].astype(BF)
        ref[r % middle, :, width:] = tail[at].astype(BF)


def expert_kernel(
    n_dp, rank, own_ref, came_ref, gate_ref, up_ref, shrink_ref, shrink2_ref, expand_ref, expand2_ref, out_ref
):
    width, hid = gate_ref.shape
    wide = shrink_ref.shape[0]
    half = n_dp // 2
    col = lax.axis_index("dp")
    order = gather_order(n_dp)
    x = jnp.concatenate([own_ref[:, :width], came_ref[:, :width]], axis=0)
    page = jnp.concatenate([own_ref[:, width:], came_ref[:, width:]], axis=0).astype(F32)[:, :1]

    def low(k, shrink):
        prod = lax.dot_general(
            x, shrink[...], (((1,), (1,)), ((), ())), preferred_element_type=F32
        )
        page_of = (col ^ k) * (wide // rank) + lax.broadcasted_iota(I32, prod.shape, 1) // rank
        return jnp.where(page == page_of.astype(F32), prod, 0.0).astype(BF)

    lows = (low(0, shrink_ref), low(1, shrink2_ref))

    def update(unit):
        at = pl.ds(pl.multiple_of(unit * hid, hid), hid)
        y = jnp.dot(lows[0], expand_ref[:, at], preferred_element_type=F32)
        return y + jnp.dot(lows[1], expand2_ref[:, at], preferred_element_type=F32)

    def put(at, y):
        out_ref[:, at : at + hid] = turned(y, col, n_dp, order, list(range(n_dp))).astype(BF)

    gate = jnp.dot(x, gate_ref[...], preferred_element_type=F32)
    up = jnp.dot(x, up_ref[...], preferred_element_type=F32)
    act = gate / (1.0 + jnp.exp(-gate))
    put(0, act)
    put(hid, act * (up + update(col)))
    if half == 2:
        put(2 * hid, update(col ^ 2))
    else:
        for i in range(half):
            unit = 2 * i + (col & 1)
            put((2 + i) * hid, jnp.where(unit == col, 0.0, update(unit)))


def down_kernel(n_dp, hid, own_ref, came_ref, down_ref, down2_ref, keep_ref, send_ref):
    col = lax.axis_index("dp")
    order = gather_order(n_dp)
    half = n_dp // 2
    each = half // 2
    split = 2 * hid * each
    rows = own_ref.shape[0]
    part = down_ref.shape[1]
    totals = [jnp.zeros((2 * rows, part), F32)] * 2
    for i, p in enumerate(order[:half]):
        ref, other = (own_ref, came_ref) if i < each else (came_ref, own_ref)
        at = (i % each) * 2 * hid
        unit = p ^ col
        start = pl.multiple_of(unit * hid, hid)
        if half == 2:
            add = other[:, split:].astype(F32)
        else:
            spot = pl.ds(pl.multiple_of(split + (unit // 2) * hid, hid), hid)
            add = ref[:, spot].astype(F32) + other[:, spot].astype(F32)
        first = ref[:, at + hid : at + 2 * hid]
        second = (ref[:, at : at + hid].astype(F32) * add).astype(BF)
        both = jnp.concatenate([first, second], axis=0)
        for k, weight in enumerate((down_ref, down2_ref)):
            totals[k] += jnp.dot(both, weight[pl.ds(start, hid), :], preferred_element_type=F32)
    for k in range(2):
        out = totals[k][:rows] + totals[k][rows:]
        out = turned(out, col, n_dp, list(range(n_dp)), order)
        keep_ref[:, k * part : (k + 1) * part] = out[: rows // 2]
        send_ref[:, (1 - k) * part : (2 - k) * part] = out[rows // 2 :].astype(BF)


def weighted(mix_ref, x_ref, first, lanes):
    mix = mix_ref[...]
    blocks, cap = x_ref.shape[:2]
    total = jnp.zeros((mix.shape[0], lanes.stop - lanes.start), F32)
    for r in range(blocks):
        x = x_ref[r, :, lanes].astype(F32)
        for c in range(cap):
            at = first + r * cap + c
            total += mix[:, at : at + 1] * x[c : c + 1]
    return total


def half_mix_kernel(part, mix_ref, kept_ref, out_ref):
    for at in range(0, out_ref.shape[1], part):
        lanes = slice(at, at + part)
        out_ref[:, lanes] = weighted(mix_ref, kept_ref, 0, lanes)


def mix_kernel(n_dp, part, mix_ref, half_ref, came_ref, out_ref):
    col = lax.axis_index("dp")
    first = came_ref.shape[0] * came_ref.shape[1]
    for p in range(n_dp):
        lanes = slice(p * part, (p + 1) * part)
        total = half_ref[:, lanes] + weighted(mix_ref, came_ref, first, lanes)
        out_ref[:, pl.ds(pl.multiple_of((p ^ col) * part, part), part)] = total.astype(BF)


def hold_kernel(x_ref, *refs):
    refs[-1][...] = x_ref[...]


def hold(x, *arrays):
    return call(
        hold_kernel,
        jax.ShapeDtypeStruct(x.shape, x.dtype),
        0,
        in_specs=[VM] + [HB] * len(arrays),
    )(x, *arrays)


def call(kernel, out_shape, n_in, limit=4 << 20, **kw):
    specs = kw.pop("in_specs", [VM] * n_in)
    outs = jax.tree.map(lambda _: VM, out_shape)
    return pl.pallas_call(
        kernel,
        out_shape=out_shape,
        in_specs=specs,
        out_specs=outs,
        compiler_params=pltpu.CompilerParams(vmem_limit_bytes=limit),
        **kw,
    )


def build(mesh):
    n_exp, n_dp = mesh.shape["expert"], mesh.shape["dp"]

    n_all = n_exp * n_dp
    both_axes = ("expert", "dp")

    def stage(blocks, axis, size, mask, dim):
        sent = [q for q in sorted(blocks) if q & mask]
        x = jnp.concatenate([blocks[q] for q in sent], axis=dim)
        came = jnp.split(swap(x, axis, size, mask), len(sent), axis=dim)
        return {**blocks, **dict(zip(sent, came))}

    def per_device(
        tokens,
        routing,
        gate_quantized,
        tenant,
        tenant_page_lookup,
        gate_weight,
        up_projection,
        down_weight,
        adapter_shrink,
        adapter_expand,
    ):
        tok_count, width = tokens.shape
        experts = tenant_page_lookup.shape[0]
        cap = tok_count // 4
        pages, rank = adapter_shrink.shape[1:3]
        hid = gate_weight.shape[2]
        hidden_all = adapter_expand.shape[3]
        part = down_weight.shape[2]
        block = experts * cap
        rows = n_dp * block
        half = n_dp // 2
        shape = jax.ShapeDtypeStruct
        middle = n_exp // 2
        kept, sent, mix = call(
            slot_kernel,
            (shape((middle, cap, width + TAIL), BF),) * 2 + (shape((tok_count, block), F32),),
            5,
            limit=None,
            in_specs=[VM, VM, VM, pl.BlockSpec(memory_space=pltpu.SMEM), VM],
        )(tokens, routing, gate_quantized, tenant, tenant_page_lookup)

        state = {}
        for i in range(middle):
            state[i], state[middle + i] = kept[i : i + 1], sent[i : i + 1]
        gate_w = gate_weight.reshape(width, hid)
        up_w = up_projection.reshape(width, hid)
        shrink_w = adapter_shrink.reshape(pages * rank, width)
        expand_w = adapter_expand.reshape(pages * rank, hidden_all)
        down_w = down_weight.reshape(-1, part)
        expand2 = swap(expand_w, "dp", n_dp, 1)
        down2 = swap(down_w, "dp", n_dp, 1)
        for mask in reversed(bits_of(n_exp)[1:]):
            state = stage(state, "expert", n_exp, mask, 0)
        even = jnp.concatenate([state[r] for r in range(0, n_exp, 2)], axis=0)
        odd = jnp.concatenate([state[r] for r in range(1, n_exp, 2)], axis=0)
        beside = swap(even, "dp", n_dp, 2)
        across = swap(odd, "expert", n_exp, 1)
        corner = swap(odd, both_axes, n_all, n_dp | 2)
        shrink2 = swap(shrink_w, "dp", n_dp, 1)
        even = hold(hold(even, expand2, down2, shrink2), gate_w, up_w)
        own = jnp.concatenate([even, across, beside, corner], axis=0)
        own = own.reshape(2 * block, width + TAIL)
        masks = bits_of(n_dp)[1:] + [1]
        for mask in masks[1:-1]:
            own = jnp.concatenate([own, swap(own, "dp", n_dp, mask)], axis=0)
        came = swap(own, "dp", n_dp, 1)
        own = hold(own, gate_w, shrink_w)
        split = 2 * hid
        parts = 1 if half == 2 else half
        packed = call(
            lambda *refs: expert_kernel(n_dp, rank, *refs),
            shape((rows, split + parts * hid), BF),
            8,
        )(own, came, gate_w, up_w, shrink_w, shrink2, expand_w, expand2)

        for mask in masks[:-2]:
            other = swap(packed, "dp", n_dp, mask)
            at = packed.shape[1] - parts * hid
            packed = jnp.concatenate(
                [packed[:, :at], other[:, :at], packed[:, at:] + other[:, at:]], axis=1
            )
        other = swap(packed, "dp", n_dp, masks[-2])
        keep, send = call(
            lambda *refs: down_kernel(n_dp, hid, *refs),
            (shape((rows // 2, 2 * part), F32), shape((rows // 2, 2 * part), BF)),
            4,
        )(packed, other, down_w, down2)

        back = swap(send, "dp", n_dp, 1)
        both = (keep + back.astype(F32)).astype(BF)
        order = gather_order(n_dp)[:half]
        each = block // 2
        state = {}
        for i, q in enumerate(order):
            for odd in range(2):
                at = i * block + odd * each
                state[q, odd] = both[at : at + each]
        for odd, far, axis, size, mask in (
            (0, 2, "dp", n_dp, 2),
            (1, 0, "expert", n_exp, 1),
            (1, 2, both_axes, n_all, n_dp | 2),
        ):
            sent = [q for q in order if (q & 2) == far]
            came = swap(jnp.concatenate([state[q, odd] for q in sent], axis=0), axis, size, mask)
            for q, x in zip(sent, jnp.split(came, len(sent), axis=0)):
                state[q, odd] = x
        home = {q: jnp.concatenate([state[q, 0], state[q, 1]], axis=0) for q in order}
        for mask in masks[1:-1]:
            home = stage(home, "dp", n_dp, mask, 0)
        home = jnp.concatenate([home[q] for q in sorted(home)], axis=1)
        home = home.reshape(n_exp, cap, n_dp * part)
        labels = list(range(0, n_exp, 2)) + list(range(1, n_exp, 2))
        state = {r: home[i : i + 1] for i, r in enumerate(labels)}
        for mask in bits_of(n_exp)[1:-1]:
            state = stage(state, "expert", n_exp, mask, 0)
        kept = jnp.concatenate([state[r] for r in range(middle)], axis=0)
        sent = jnp.concatenate([state[r] for r in range(middle, n_exp)], axis=0)
        came = swap(sent, "expert", n_exp, middle)
        mixed = call(
            lambda *refs: half_mix_kernel(part, *refs),
            shape((tok_count, n_dp * part), F32),
            2,
            cost_estimate=pl.CostEstimate(
                flops=2 * tok_count * middle * cap * n_dp * part,
                bytes_accessed=4 * tok_count * n_dp * part,
                transcendentals=0,
            ),
        )(mix, kept)
        return call(
            lambda *refs: mix_kernel(n_dp, part, *refs),
            shape((tok_count, n_dp * part), BF),
            3,
        )(mix, mixed, came)

    return per_device


def solution(mesh):
    row = ("group", "expert", "dp")
    return jax.shard_map(
        build(mesh),
        mesh=mesh,
        in_specs=(
            P(row, None),
            P(row, None),
            P(row, None),
            P(row),
            P(),
            P("expert", None, "dp"),
            P("expert", None, "dp"),
            P("expert", None, "dp"),
            P("expert", "dp", None, None),
            P("expert", "dp", None, None),
        ),
        out_specs=P(row, None),
        check_vma=False,
    )
```

```python
import jax
import jax.numpy as jnp
from jax import lax
from jax.experimental import pallas as pl
from jax.experimental.pallas import tpu as pltpu
from jax.sharding import PartitionSpec as P

BF = jnp.bfloat16
F32 = jnp.float32
I32 = jnp.int32
TAIL = 128
VM = pl.BlockSpec(memory_space=pltpu.VMEM)
HB = pl.BlockSpec(memory_space=pl.ANY)


def swap(x, axis, size, mask):
    return lax.ppermute(x, axis, [(i, i ^ mask) for i in range(size)])


def bits_of(size):
    return [1 << b for b in range(size.bit_length() - 1)]


def gather_order(size):
    order = [0]
    for mask in bits_of(size)[1:] + [1]:
        order = order + [q ^ mask for q in order]
    return order


def turned(x, col, size, names_in, names_out):
    rows = x.shape[0] // size
    block = {q: x[i * rows : (i + 1) * rows] for i, q in enumerate(names_in)}
    for mask in bits_of(size):
        here = (col & mask) != 0
        block = {q: jnp.where(here, block[q ^ mask], block[q]) for q in range(size)}
    return jnp.concatenate([block[q] for q in names_out], axis=0)


def slot_kernel(
    tok_ref, routing_ref, gate_ref, tenant_ref, lookup_ref, keep_ref, send_ref, mix_ref
):
    tok_count, width = tok_ref.shape
    experts, tenants = lookup_ref.shape
    slots = mix_ref.shape[1]
    cap = slots // experts
    topk = routing_ref.shape[1]
    mine = lax.axis_index("expert")
    lane = lax.broadcasted_iota(I32, (tok_count, slots), 1)
    expert_of = (lane // cap) ^ mine
    routing = routing_ref[...]
    quant = gate_ref[...].astype(F32) * (1.0 / 32768.0)
    assign = jnp.zeros((tok_count, slots), F32)
    coef = jnp.zeros((tok_count, slots), F32)
    for k in range(topk):
        match = routing[:, k : k + 1] == expert_of
        assign = jnp.where(match, 1.0, assign)
        coef = jnp.where(match, quant[:, k : k + 1], coef)
    below = lax.broadcasted_iota(I32, (tok_count, tok_count), 0) > lax.broadcasted_iota(
        I32, (tok_count, tok_count), 1
    )
    slot_rank = jnp.dot(
        jnp.where(below, 1.0, 0.0).astype(BF), assign.astype(BF), preferred_element_type=F32
    )
    place = jnp.where(slot_rank == (lane % cap).astype(F32), assign, 0.0)
    mix_ref[...] = place * coef
    row = lax.broadcasted_iota(I32, (tok_count, tenants), 0)
    who = jnp.zeros((tok_count, tenants), I32)
    for t in range(tok_count):
        who = jnp.where(row == t, tenant_ref[t], who)
    hot = jnp.where(lax.broadcasted_iota(I32, (tok_count, tenants), 1) == who, 1.0, 0.0)
    pages = lax.dot_general(
        hot.astype(BF),
        lookup_ref[...].astype(F32).astype(BF),
        (((1,), (1,)), ((), ())),
        preferred_element_type=F32,
    )
    pick = jnp.where(
        lax.broadcasted_iota(I32, (experts, slots), 0)
        == (lax.broadcasted_iota(I32, (experts, slots), 1) // cap) ^ mine,
        1.0,
        0.0,
    )
    page = place * jnp.dot(pages.astype(BF), pick.astype(BF), preferred_element_type=F32)
    by_token = (((0,), (0,)), ((), ()))
    rows = lax.dot_general(place.astype(BF), tok_ref[...], by_token, preferred_element_type=F32)
    tail = lax.dot_general(
        page.astype(BF), jnp.ones((tok_count, TAIL), BF), by_token, preferred_element_type=F32
    )
    for r in range(experts):
        middle = experts // 2
        ref = send_ref if r >= middle else keep_ref
        at = slice(r * cap, (r + 1) * cap)
        ref[r % middle, :, :width] = rows[at].astype(BF)
        ref[r % middle, :, width:] = tail[at].astype(BF)


def rows_of(own_ref, came_ref, width):
    return jnp.concatenate([own_ref[:, :width], came_ref[:, :width]], axis=0)


def shrink_kernel(n_dp, rank, own_ref, came_ref, shrink_ref, out_ref):
    wide, width = shrink_ref.shape
    col = lax.axis_index("dp")
    x = rows_of(own_ref, came_ref, width)
    page = jnp.concatenate([own_ref[:, width:], came_ref[:, width:]], axis=0).astype(F32)[:, :1]
    prod = lax.dot_general(
        x, shrink_ref[...], (((1,), (1,)), ((), ())), preferred_element_type=F32
    )
    page_of = col * (wide // rank) + lax.broadcasted_iota(I32, prod.shape, 1) // rank
    masked = jnp.where(page == page_of.astype(F32), prod, 0.0)
    out_ref[...] = turned(masked, col, n_dp, gather_order(n_dp), list(range(n_dp))).astype(BF)


def expert_kernel(n_dp, own_ref, came_ref, gate_ref, up_ref, out_ref):
    width, hid = gate_ref.shape
    col = lax.axis_index("dp")
    x = rows_of(own_ref, came_ref, width)
    gate = jnp.dot(x, gate_ref[...], preferred_element_type=F32)
    up = jnp.dot(x, up_ref[...], preferred_element_type=F32)
    act = gate / (1.0 + jnp.exp(-gate))
    for i, y in enumerate((act, up)):
        y = turned(y, col, n_dp, gather_order(n_dp), list(range(n_dp)))
        out_ref[:, i * hid : (i + 1) * hid] = y


def grow_kernel(n_dp, low_ref, low2_ref, expand_ref, expand2_ref, act_ref, out_ref):
    col = lax.axis_index("dp")
    hid = act_ref.shape[1] // 2
    half = n_dp // 2

    def update(unit):
        at = pl.ds(pl.multiple_of(unit * hid, hid), hid)
        y = jnp.dot(low_ref[...], expand_ref[:, at], preferred_element_type=F32)
        return y + jnp.dot(low2_ref[...], expand2_ref[:, at], preferred_element_type=F32)

    act = act_ref[:, :hid]
    out_ref[:, :hid] = act.astype(BF)
    out_ref[:, hid : 2 * hid] = (act * (act_ref[:, hid:] + update(col))).astype(BF)
    if half == 2:
        out_ref[:, 2 * hid :] = update(col ^ 2).astype(BF)
    else:
        for i in range(half):
            unit = 2 * i + (col & 1)
            y = jnp.where(unit == col, 0.0, update(unit))
            out_ref[:, (2 + i) * hid : (3 + i) * hid] = y.astype(BF)


def down_kernel(n_dp, hid, own_ref, came_ref, down_ref, down2_ref, keep_ref, send_ref):
    col = lax.axis_index("dp")
    order = gather_order(n_dp)
    half = n_dp // 2
    each = half // 2
    split = 2 * hid * each
    rows = own_ref.shape[0]
    part = down_ref.shape[1]
    totals = [jnp.zeros((2 * rows, part), F32)] * 2
    for i, p in enumerate(order[:half]):
        ref, other = (own_ref, came_ref) if i < each else (came_ref, own_ref)
        at = (i % each) * 2 * hid
        unit = p ^ col
        start = pl.multiple_of(unit * hid, hid)
        if half == 2:
            add = other[:, split:].astype(F32)
        else:
            spot = pl.ds(pl.multiple_of(split + (unit // 2) * hid, hid), hid)
            add = ref[:, spot].astype(F32) + other[:, spot].astype(F32)
        first = ref[:, at + hid : at + 2 * hid]
        second = (ref[:, at : at + hid].astype(F32) * add).astype(BF)
        both = jnp.concatenate([first, second], axis=0)
        for k, weight in enumerate((down_ref, down2_ref)):
            totals[k] += jnp.dot(both, weight[pl.ds(start, hid), :], preferred_element_type=F32)
    for k in range(2):
        out = totals[k][:rows] + totals[k][rows:]
        out = turned(out, col, n_dp, list(range(n_dp)), order)
        keep_ref[:, k * part : (k + 1) * part] = out[: rows // 2]
        send_ref[:, (1 - k) * part : (2 - k) * part] = out[rows // 2 :].astype(BF)


def weighted(mix_ref, x_ref, first, lanes):
    mix = mix_ref[...]
    blocks, cap = x_ref.shape[:2]
    total = jnp.zeros((mix.shape[0], lanes.stop - lanes.start), F32)
    for r in range(blocks):
        x = x_ref[r, :, lanes].astype(F32)
        for c in range(cap):
            at = first + r * cap + c
            total += mix[:, at : at + 1] * x[c : c + 1]
    return total


def half_mix_kernel(part, mix_ref, kept_ref, out_ref):
    for at in range(0, out_ref.shape[1], part):
        lanes = slice(at, at + part)
        out_ref[:, lanes] = weighted(mix_ref, kept_ref, 0, lanes)


def mix_kernel(n_dp, part, mix_ref, half_ref, came_ref, out_ref):
    col = lax.axis_index("dp")
    first = came_ref.shape[0] * came_ref.shape[1]
    for p in range(n_dp):
        lanes = slice(p * part, (p + 1) * part)
        total = half_ref[:, lanes] + weighted(mix_ref, came_ref, first, lanes)
        out_ref[:, pl.ds(pl.multiple_of((p ^ col) * part, part), part)] = total.astype(BF)


def hold_kernel(x_ref, *refs):
    refs[-1][...] = x_ref[...]


def hold(x, *arrays):
    return call(
        hold_kernel,
        jax.ShapeDtypeStruct(x.shape, x.dtype),
        0,
        in_specs=[VM] + [HB] * len(arrays),
    )(x, *arrays)


def call(kernel, out_shape, n_in, limit=4 << 20, **kw):
    specs = kw.pop("in_specs", [VM] * n_in)
    outs = jax.tree.map(lambda _: VM, out_shape)
    return pl.pallas_call(
        kernel,
        out_shape=out_shape,
        in_specs=specs,
        out_specs=outs,
        compiler_params=pltpu.CompilerParams(vmem_limit_bytes=limit),
        **kw,
    )


def build(mesh):
    n_exp, n_dp = mesh.shape["expert"], mesh.shape["dp"]

    n_all = n_exp * n_dp
    both_axes = ("expert", "dp")

    def stage(blocks, axis, size, mask, dim):
        sent = [q for q in sorted(blocks) if q & mask]
        x = jnp.concatenate([blocks[q] for q in sent], axis=dim)
        came = jnp.split(swap(x, axis, size, mask), len(sent), axis=dim)
        return {**blocks, **dict(zip(sent, came))}

    def per_device(
        tokens,
        routing,
        gate_quantized,
        tenant,
        tenant_page_lookup,
        gate_weight,
        up_projection,
        down_weight,
        adapter_shrink,
        adapter_expand,
    ):
        tok_count, width = tokens.shape
        experts = tenant_page_lookup.shape[0]
        cap = tok_count // 4
        pages, rank = adapter_shrink.shape[1:3]
        hid = gate_weight.shape[2]
        hidden_all = adapter_expand.shape[3]
        part = down_weight.shape[2]
        block = experts * cap
        rows = n_dp * block
        half = n_dp // 2
        shape = jax.ShapeDtypeStruct
        middle = n_exp // 2
        kept, sent, mix = call(
            slot_kernel,
            (shape((middle, cap, width + TAIL), BF),) * 2 + (shape((tok_count, block), F32),),
            5,
            limit=None,
            in_specs=[VM, VM, VM, pl.BlockSpec(memory_space=pltpu.SMEM), VM],
        )(tokens, routing, gate_quantized, tenant, tenant_page_lookup)

        state = {}
        for i in range(middle):
            state[i], state[middle + i] = kept[i : i + 1], sent[i : i + 1]
        gate_w = gate_weight.reshape(width, hid)
        up_w = up_projection.reshape(width, hid)
        shrink_w = adapter_shrink.reshape(pages * rank, width)
        expand_w = adapter_expand.reshape(pages * rank, hidden_all)
        down_w = down_weight.reshape(-1, part)
        expand2 = swap(expand_w, "dp", n_dp, 1)
        down2 = swap(down_w, "dp", n_dp, 1)
        for mask in reversed(bits_of(n_exp)[1:]):
            state = stage(state, "expert", n_exp, mask, 0)
        even = jnp.concatenate([state[r] for r in range(0, n_exp, 2)], axis=0)
        odd = jnp.concatenate([state[r] for r in range(1, n_exp, 2)], axis=0)
        across = swap(odd, "expert", n_exp, 1)
        corner = swap(odd, both_axes, n_all, n_dp | 2)
        beside = swap(even, "dp", n_dp, 2)
        even = hold(hold(even, expand2, down2), gate_w, up_w)
        own = jnp.concatenate([even, across, beside, corner], axis=0)
        own = own.reshape(2 * block, width + TAIL)
        masks = bits_of(n_dp)[1:] + [1]
        for mask in masks[1:-1]:
            own = jnp.concatenate([own, swap(own, "dp", n_dp, mask)], axis=0)
        came = swap(own, "dp", n_dp, 1)
        own = hold(own, gate_w, shrink_w, expand_w)
        low = call(
            lambda *refs: shrink_kernel(n_dp, rank, *refs), shape((rows, pages * rank), BF), 3
        )(own, came, shrink_w)
        low2 = swap(low, "dp", n_dp, 1)
        acts = call(
            lambda *refs: expert_kernel(n_dp, *refs),
            shape((rows, 2 * hid), F32),
            4,
            cost_estimate=pl.CostEstimate(
                flops=4 * rows * width * hid, bytes_accessed=4 * width * hid, transcendentals=0
            ),
        )(own, came, gate_w, up_w)
        split = 2 * hid
        parts = 1 if half == 2 else half
        packed = call(
            lambda *refs: grow_kernel(n_dp, *refs), shape((rows, split + parts * hid), BF), 5
        )(low, low2, expand_w, expand2, acts)

        for mask in masks[:-2]:
            other = swap(packed, "dp", n_dp, mask)
            at = packed.shape[1] - parts * hid
            packed = jnp.concatenate(
                [packed[:, :at], other[:, :at], packed[:, at:] + other[:, at:]], axis=1
            )
        other = swap(packed, "dp", n_dp, masks[-2])
        keep, send = call(
            lambda *refs: down_kernel(n_dp, hid, *refs),
            (shape((rows // 2, 2 * part), F32), shape((rows // 2, 2 * part), BF)),
            4,
        )(packed, other, down_w, down2)

        back = swap(send, "dp", n_dp, 1)
        both = (keep + back.astype(F32)).astype(BF)
        order = gather_order(n_dp)[:half]
        each = block // 2
        state = {}
        for i, q in enumerate(order):
            for odd in range(2):
                at = i * block + odd * each
                state[q, odd] = both[at : at + each]
        for odd, far, axis, size, mask in (
            (0, 2, "dp", n_dp, 2),
            (1, 0, "expert", n_exp, 1),
            (1, 2, both_axes, n_all, n_dp | 2),
        ):
            sent = [q for q in order if (q & 2) == far]
            came = swap(jnp.concatenate([state[q, odd] for q in sent], axis=0), axis, size, mask)
            for q, x in zip(sent, jnp.split(came, len(sent), axis=0)):
                state[q, odd] = x
        home = {q: jnp.concatenate([state[q, 0], state[q, 1]], axis=0) for q in order}
        for mask in masks[1:-1]:
            home = stage(home, "dp", n_dp, mask, 0)
        home = jnp.concatenate([home[q] for q in sorted(home)], axis=1)
        home = home.reshape(n_exp, cap, n_dp * part)
        labels = list(range(0, n_exp, 2)) + list(range(1, n_exp, 2))
        state = {r: home[i : i + 1] for i, r in enumerate(labels)}
        for mask in bits_of(n_exp)[1:-1]:
            state = stage(state, "expert", n_exp, mask, 0)
        kept = jnp.concatenate([state[r] for r in range(middle)], axis=0)
        sent = jnp.concatenate([state[r] for r in range(middle, n_exp)], axis=0)
        came = swap(sent, "expert", n_exp, middle)
        mixed = call(
            lambda *refs: half_mix_kernel(part, *refs),
            shape((tok_count, n_dp * part), F32),
            2,
            cost_estimate=pl.CostEstimate(
                flops=2 * tok_count * middle * cap * n_dp * part,
                bytes_accessed=4 * tok_count * n_dp * part,
                transcendentals=0,
            ),
        )(mix, kept)
        return call(
            lambda *refs: mix_kernel(n_dp, part, *refs),
            shape((tok_count, n_dp * part), BF),
            3,
        )(mix, mixed, came)

    return per_device


def solution(mesh):
    row = ("group", "expert", "dp")
    return jax.shard_map(
        build(mesh),
        mesh=mesh,
        in_specs=(
            P(row, None),
            P(row, None),
            P(row, None),
            P(row),
            P(),
            P("expert", None, "dp"),
            P("expert", None, "dp"),
            P("expert", None, "dp"),
            P("expert", "dp", None, None),
            P("expert", "dp", None, None),
        ),
        out_specs=P(row, None),
        check_vma=False,
    )
```
